256 devices in a mesh: dp: 16 (over x, y), expert: 16 (over z, core).
Axes of the slice: x: 4, y: 4, z: 8, core: 2. Of those that a mesh axis runs over, the one named last changes fastest.
Arguments:
- tokens: bfloat16 [40960, 2048], P(('dp', 'expert')), may hold values from -24 to 24
- out_grads: bfloat16 [40960, 2048], P(('dp', 'expert')), may hold values from -6 to 6
- expert_ids: int32 [40960, 1], P(('dp', 'expert')), may hold values from 0 to 15; in each aligned block of 160 rows (0 to 159, 160 to 319, ...) at most 30 rows name the same one
- w_gate_up: bfloat16 [16, 2048, 1536], P('expert'), may hold values from -0.125 to 0.125
- w_down_t: bfloat16 [16, 2048, 768], P('expert'), may hold values from -0.21875 to 0.21875
Outputs:
- token_grads: bfloat16 [40960, 2048], P(('dp', 'expert'))
- grad_gate_up: bfloat16 [16, 2048, 1536], P('expert', 'dp')
- grad_down_t: bfloat16 [16, 2048, 768], P('expert', 'dp')
The draws below stay inside these ranges and needn't reach their ends.
Inputs may be any that keep to these rules, and one draw needn't show every extreme that they name: `expert_ids`: within one device's 160 rows (an aligned block) no expert is named more than 30 times; in some blocks one expert is named exactly 30 times.
All inputs are finite; a program needn't handle non-finite values.
Results may differ from the reference program's by a relative error of at most 0.02.
Values may be sent and summed in bfloat16 or wider, within the bound.
No kernel may reach another device: no remote copies, remote signals or barrier semaphores. Data moves between devices by JAX's collectives and lax.ppermute only.
A program may use at most 128 MiB of HBM per device.

```python
import math
import jax
import jax.numpy as jnp
import numpy as np
from jax import lax

D = 2048
FF = 768
TOK_DEV = 160
EXPERTS = 16
CAP = 30
TOKENS = 40960
N_DP = 16
N_EXPERT = 16


def with_spikes(drawn, own_key, source, target, blocks, factor):
    def block_of(axis_at):
        return (jnp.arange(drawn.shape[axis_at]) // (drawn.shape[axis_at] // blocks)).reshape((-1,) + (1,) * (drawn.ndim - 1 - axis_at))

    near = jax.random.permutation(own_key, blocks)[block_of(target)]
    other_side = (block_of(target) + blocks // 2) % blocks
    return jnp.where((block_of(source) == near) | (block_of(source) == other_side), factor * drawn, drawn)


def block_levels(rng, extent, shards, low, top_value):
    gain, own = 1.0, jax.random.fold_in(rng, 6)
    for dim, blocks in shards:
        steps = jnp.exp(jax.random.uniform(jax.random.fold_in(own, dim), (blocks,), jnp.float32, low / len(shards), top_value / len(shards)))
        gain = gain * jnp.repeat(steps, extent[dim] // blocks).reshape([-1 if axis == dim else 1 for axis in range(len(extent))])
    return gain


def routed_block(own_key, own, number, rows, amount, top, bound, skew):
    order = jax.random.permutation(own_key, amount)
    crowded, ordinary = load_shares(amount, rows * top, bound, skew, True), load_shares(amount, rows * top, bound, skew, False)
    places = jnp.arange(amount)

    def named(lengths, offset_by):
        used = int((lengths > 0).sum())
        fixed = max(1, used // 4)
        moved = fixed + (places - fixed + offset_by * (used - fixed)) % max(1, amount - fixed)
        return jnp.zeros((amount,), jnp.int32).at[order[jnp.where(places < fixed, places, moved)]].set(jnp.asarray(lengths, jnp.int32))

    lengths = jnp.where(number % 4 == 0, named(crowded, number // 4), named(ordinary, number - number // 4 - 1))
    mixed = jax.random.permutation(jax.random.fold_in(own, 3), amount)
    source_of, taker = mixed[0:amount // 2 * 2:2], mixed[1:amount // 2 * 2:2]
    slack = jnp.minimum(lengths[source_of] - 1, bound - lengths[taker]) // 2
    slack = jnp.where((source_of == order[0]) | (taker == order[0]) | (lengths[taker] == 0), 0, jnp.maximum(slack, 0))
    moved = jax.random.randint(jax.random.fold_in(own, 4), (amount // 2,), 0, 1 << 20) % (slack + 1)
    lengths = lengths.at[source_of].add(-moved).at[taker].add(moved)
    members = jnp.searchsorted(jnp.cumsum(lengths), jnp.arange(rows * top), side="right").astype(jnp.int32)
    listing = members.reshape(top, rows).T
    listing = listing[jax.random.permutation(jax.random.fold_in(own, 1), rows)]
    offset_by = jax.random.randint(jax.random.fold_in(own, 2), (rows, 1), 0, top)
    return jnp.take_along_axis(listing, (jnp.arange(top)[None, :] + offset_by) % top, axis=1)


def load_shares(count, total, limit, lean, full):
    portions = [(1 << 20) // math.isqrt(rank ** lean) + 1 for rank in range(1, count + 1)]
    largest = limit if full else min(limit, max(-(-total // count), total * portions[0] // sum(portions)))
    least = 1 if total - largest >= count - 1 else 0
    given, spare = [largest] + [least] * (count - 1), total - largest - least * (count - 1)
    while spare > 0:
        movable = [i for i in range(1, count) if given[i] < largest] or [i for i in range(1, count) if given[i] < limit]
        mass, left = sum([portions[i] for i in movable]), spare
        for i in movable:
            extra = min(limit - given[i], max(1, left * portions[i] // mass), spare)
            given[i] = given[i] + extra
            spare = spare - extra
    return np.array(given)


def centred(own_key, extent, spread, bound, cuts=(), held_as=jnp.bfloat16):
    level = block_levels(own_key, extent, cuts, -0.22, 0.18) if cuts else 1.0
    values = jax.random.normal(own_key, extent, jnp.float32) * spread * level
    return jnp.minimum(jnp.maximum(values, -bound), bound).astype(held_as)


def heavy_noise(own_key, extent, spread, most, cuts, heavy, kind=jnp.bfloat16):
    array = spread * jax.random.normal(own_key, extent, jnp.float32)
    if cuts:
        array = array * block_levels(own_key, extent, cuts, -0.22, 0.18)
    return jnp.clip(with_spikes(array, jax.random.fold_in(own_key, 3), *heavy), -most, most).astype(kind)


def setup_inputs(seed: int = 0) -> dict:
    seeds = jax.random.split(jax.random.key(seed), 6)
    tokens = heavy_noise(seeds[0], (TOKENS, D), 1.0, 24.0, ((0, 256),), (0, 1, 256, 6.0))
    out_grads = centred(seeds[1], (TOKENS, D), 1.0, 6.0, ((0, 256),))
    expert_ids_keys = jax.random.split(jax.random.fold_in(seeds[2], 1), TOKENS // TOK_DEV)
    expert_ids_turns = jax.random.permutation(jax.random.fold_in(seeds[2], 3), TOKENS // TOK_DEV)
    expert_ids = jax.vmap(lambda own, number: routed_block(jax.random.fold_in(seeds[2], 2), own, number, TOK_DEV, EXPERTS, 1, CAP, 2))(expert_ids_keys, expert_ids_turns).reshape((TOKENS, 1))
    w_gate_up = centred(seeds[3], (EXPERTS, D, 2 * FF), D ** -0.5, 0.125, ((0, 16),))
    w_down_t = centred(seeds[4], (EXPERTS, D, FF), FF ** -0.5, 0.21875, ((0, 16),))
    return {"tokens": tokens, "out_grads": out_grads, "expert_ids": expert_ids, "w_gate_up": w_gate_up, "w_down_t": w_down_t}


def reference(tokens, out_grads, expert_ids, w_gate_up, w_down_t):
    num_experts = N_EXPERT
    capacity = CAP
    routed = expert_ids[:, 0].reshape(N_DP, num_experts, TOK_DEV)
    inputs_x = tokens.reshape(N_DP, num_experts, TOK_DEV, D)
    inputs_dy = out_grads.reshape(N_DP, num_experts, TOK_DEV, D)

    def group(carry, group_inputs):
        group_x, group_dy, group_ids = group_inputs
        onehot = (group_ids[:, :, None] == jnp.arange(num_experts, dtype=jnp.int32)[None, None, :]).astype(jnp.int32)
        ranks = (jnp.cumsum(onehot, axis=1) - 1).astype(jnp.int32)
        slots = jnp.sum(ranks * onehot, axis=2).astype(jnp.int32)
        slot_range = jnp.arange(capacity, dtype=jnp.int32)

        def expert(grad_acc, expert_inputs):
            which, wgu, wdown = expert_inputs
            select = ((group_ids == which)[:, None, :] & (slots[:, None, :] == slot_range[None, :, None])).astype(jnp.float32)
            rows_x = jnp.einsum('jct,jtd->jcd', select, group_x.astype(jnp.float32)).reshape(num_experts * capacity, D).astype(jnp.bfloat16)
            rows_dy = jnp.einsum('jct,jtd->jcd', select, group_dy.astype(jnp.float32)).reshape(num_experts * capacity, D).astype(jnp.bfloat16)
            gate_up = jnp.dot(rows_x, wgu, preferred_element_type=jnp.float32)
            gate = gate_up[:, :FF]
            upper = gate_up[:, FF:]
            sigmoid_gate = jax.nn.sigmoid(gate)
            silu_gate = gate * sigmoid_gate
            hidden = (silu_gate * upper).astype(jnp.bfloat16)
            dhidden = jnp.dot(rows_dy, wdown, preferred_element_type=jnp.float32)
            dgate = dhidden * upper * sigmoid_gate * (1.0 + gate * (1.0 - sigmoid_gate))
            dupper = dhidden * silu_gate
            dgate_up = jnp.concatenate([dgate, dupper], axis=1).astype(jnp.bfloat16)
            drows = lax.dot_general(dgate_up, wgu, (((1,), (1,)), ((), ())), preferred_element_type=jnp.float32).astype(jnp.bfloat16)
            back = drows.reshape(num_experts, capacity, D).astype(jnp.float32)
            grad_acc = grad_acc + jnp.einsum('jct,jcd->jtd', select, back)
            first = lax.dot_general(rows_x, dgate_up, (((0,), (0,)), ((), ())), preferred_element_type=jnp.float32)
            second = lax.dot_general(rows_dy, hidden, (((0,), (0,)), ((), ())), preferred_element_type=jnp.float32)
            partial_term = jnp.concatenate([first, second], axis=1).astype(jnp.bfloat16)
            return grad_acc, partial_term

        start = jnp.zeros((num_experts, TOK_DEV, D), jnp.float32)
        group_grads, partials = lax.scan(expert, start, (jnp.arange(EXPERTS, dtype=jnp.int32), w_gate_up, w_down_t))
        carry = carry + partials.astype(jnp.float32)
        return carry, group_grads.astype(jnp.bfloat16)

    total = jnp.zeros((EXPERTS, D, 3 * FF), jnp.float32)
    total, token_parts = lax.scan(group, total, (inputs_x, inputs_dy, routed))
    token_grads = token_parts.reshape(TOKENS, D)
    return token_grads, total[:, :, :2 * FF].astype(jnp.bfloat16), total[:, :, 2 * FF:].astype(jnp.bfloat16)
```

```python
import jax
import jax.numpy as jnp
from jax import lax
from jax.sharding import PartitionSpec as P

SLOTS = 32


def slot_table(routed, num_experts):
    rows = routed.shape[0]
    places = jnp.arange(rows, dtype=jnp.int32)
    same = (routed[:, None] == routed[None, :]) & (places[:, None] < places[None, :])
    slots = jnp.sum(same.astype(jnp.int32), axis=0)
    target = routed * SLOTS + slots
    spots = jnp.arange(num_experts * SLOTS, dtype=jnp.int32)
    return (spots[:, None] == target[None, :]).astype(jnp.bfloat16)


def local(tokens, out_grads, expert_ids, w_gate_up, w_down_t):
    num_experts = lax.axis_size("expert")
    width = tokens.shape[1]
    ff = w_down_t.shape[2]
    dispatch = slot_table(expert_ids[:, 0], num_experts)

    def send(rows):
        slots = jnp.dot(dispatch, rows, preferred_element_type=jnp.float32).astype(jnp.bfloat16)
        slots = slots.reshape(num_experts, SLOTS, width)
        got = lax.all_to_all(slots, "expert", split_axis=0, concat_axis=0, tiled=True)
        return got.reshape(num_experts * SLOTS, width)

    rows_x = send(tokens)
    rows_dy = send(out_grads)
    w_in = w_gate_up[0]
    w_out = w_down_t[0]
    gate_up = jnp.dot(rows_x, w_in, preferred_element_type=jnp.float32)
    gate = gate_up[:, :ff]
    upper = gate_up[:, ff:]
    sig = jax.nn.sigmoid(gate)
    silu = gate * sig
    hidden = (silu * upper).astype(jnp.bfloat16)
    dhidden = jnp.dot(rows_dy, w_out, preferred_element_type=jnp.float32)
    dgate = dhidden * upper * sig * (1.0 + gate * (1.0 - sig))
    dupper = dhidden * silu
    dgate_up = jnp.concatenate([dgate, dupper], axis=1).astype(jnp.bfloat16)
    drows = lax.dot_general(
        dgate_up, w_in, (((1,), (1,)), ((), ())), preferred_element_type=jnp.float32
    ).astype(jnp.bfloat16)
    returned = lax.all_to_all(
        drows.reshape(num_experts, SLOTS, width), "expert", split_axis=0, concat_axis=0, tiled=True
    ).reshape(num_experts * SLOTS, width)
    token_grads = lax.dot_general(
        dispatch, returned, (((0,), (0,)), ((), ())), preferred_element_type=jnp.float32
    ).astype(jnp.bfloat16)
    first = lax.dot_general(
        rows_x, dgate_up, (((0,), (0,)), ((), ())), preferred_element_type=jnp.float32
    ).astype(jnp.bfloat16)
    second = lax.dot_general(
        rows_dy, hidden, (((0,), (0,)), ((), ())), preferred_element_type=jnp.float32
    ).astype(jnp.bfloat16)
    grad_gate_up = lax.psum_scatter(first, "dp", scatter_dimension=0, tiled=True)[None]
    grad_down_t = lax.psum_scatter(second, "dp", scatter_dimension=0, tiled=True)[None]
    return (token_grads, grad_gate_up, grad_down_t)


def solution(mesh):
    return jax.shard_map(
        local,
        mesh=mesh,
        in_specs=(
            P(("dp", "expert"), None),
            P(("dp", "expert"), None),
            P(("dp", "expert"), None),
            P("expert", None, None),
            P("expert", None, None),
        ),
        out_specs=(P(("dp", "expert"), None), P("expert", "dp", None), P("expert", "dp", None)),
        check_vma=False,
    )
```

```python
import jax
import jax.numpy as jnp
from jax import lax
from jax.sharding import PartitionSpec as P

SLOTS = 32


def slot_table(routed, num_experts):
    rows = routed.shape[0]
    places = jnp.arange(rows, dtype=jnp.int32)
    same = (routed[:, None] == routed[None, :]) & (places[:, None] < places[None, :])
    slots = jnp.sum(same.astype(jnp.int32), axis=0)
    target = routed * SLOTS + slots
    spots = jnp.arange(num_experts * SLOTS, dtype=jnp.int32)
    return (spots[:, None] == target[None, :]).astype(jnp.bfloat16)


def pair_perm(axis, odd):
    def mate(i):
        return (i ^ 1) if not odd else (3 - i)

    return [
        (x * 4 + y, mate(x) * 4 + y if axis == 0 else x * 4 + mate(y))
        for x in range(4)
        for y in range(4)
    ]


def scatter_sum(partial):
    me = lax.axis_index("dp")
    at = (me // 4, me % 4)
    cols = partial.shape[1]
    rows = partial.shape[0] // 64
    view = partial.reshape(4, 4, 4, rows, cols)

    def half(block, axis, first_odd, step):
        i = at[axis]
        if step == 0:
            if first_odd:
                low, high = lax.slice_in_dim(block, 0, 2, 1, axis), lax.slice_in_dim(block, 2, 4, 1, axis)
                mine_low = i < 2
            else:
                low, high = lax.slice_in_dim(block, 0, 4, 3, axis), lax.slice_in_dim(block, 1, 3, 1, axis)
                mine_low = (i == 0) | (i == 3)
        else:
            low, high = lax.slice_in_dim(block, 0, 1, 1, axis), lax.slice_in_dim(block, 1, 2, 1, axis)
            mine_low = (i % 2 == 0) if first_odd else (i < 2)
        return jnp.where(mine_low, high, low), jnp.where(mine_low, low, high)

    plans = (
        ((0, False), (0, True), (1, False), (1, True)),
        ((0, True), (0, False), (1, True), (1, False)),
        ((1, False), (1, True), (0, False), (0, True)),
        ((1, True), (1, False), (0, True), (0, False)),
    )
    blocks = [view[:, :, f] for f in range(4)]
    for step in range(4):
        out = []
        for block, plan in zip(blocks, plans):
            axis, odd = plan[step]
            first_odd = plan[step - step % 2][1]
            give, keep = half(block, axis, first_odd, step % 2)
            got = lax.ppermute(give, "dp", pair_perm(axis, odd))
            out.append((keep.astype(jnp.float32) + got.astype(jnp.float32)).astype(jnp.bfloat16))
        blocks = out
    return jnp.concatenate([b.reshape(rows, cols) for b in blocks], axis=0)


def local(tokens, out_grads, expert_ids, w_gate_up, w_down_t):
    num_experts = lax.axis_size("expert")
    width = tokens.shape[1]
    ff = w_down_t.shape[2]
    dispatch = slot_table(expert_ids[:, 0], num_experts)

    def send(rows):
        slots = jnp.dot(dispatch, rows, preferred_element_type=jnp.float32).astype(jnp.bfloat16)
        slots = slots.reshape(num_experts, SLOTS, width)
        got = lax.all_to_all(slots, "expert", split_axis=0, concat_axis=0, tiled=True)
        return got.reshape(num_experts * SLOTS, width)

    rows_x = send(tokens)
    rows_dy = send(out_grads)
    w_in = w_gate_up[0]
    w_out = w_down_t[0]
    gate_up = jnp.dot(rows_x, w_in, preferred_element_type=jnp.float32)
    gate = gate_up[:, :ff]
    upper = gate_up[:, ff:]
    sig = jax.nn.sigmoid(gate)
    silu = gate * sig
    hidden = (silu * upper).astype(jnp.bfloat16)
    dhidden = jnp.dot(rows_dy, w_out, preferred_element_type=jnp.float32)
    dgate = dhidden * upper * sig * (1.0 + gate * (1.0 - sig))
    dupper = dhidden * silu
    dgate_up = jnp.concatenate([dgate, dupper], axis=1).astype(jnp.bfloat16)
    drows = lax.dot_general(
        dgate_up, w_in, (((1,), (1,)), ((), ())), preferred_element_type=jnp.float32
    ).astype(jnp.bfloat16)
    returned = lax.all_to_all(
        drows.reshape(num_experts, SLOTS, width), "expert", split_axis=0, concat_axis=0, tiled=True
    ).reshape(num_experts * SLOTS, width)
    token_grads = lax.dot_general(
        dispatch, returned, (((0,), (0,)), ((), ())), preferred_element_type=jnp.float32
    ).astype(jnp.bfloat16)
    first = lax.dot_general(
        rows_x, dgate_up, (((0,), (0,)), ((), ())), preferred_element_type=jnp.float32
    ).astype(jnp.bfloat16)
    second = lax.dot_general(
        rows_dy, hidden, (((0,), (0,)), ((), ())), preferred_element_type=jnp.float32
    ).astype(jnp.bfloat16)
    summed = scatter_sum(jnp.concatenate([first, second], axis=1))
    return (token_grads, summed[None, :, : 2 * ff], summed[None, :, 2 * ff :])


def solution(mesh):
    return jax.shard_map(
        local,
        mesh=mesh,
        in_specs=(
            P(("dp", "expert"), None),
            P(("dp", "expert"), None),
            P(("dp", "expert"), None),
            P("expert", None, None),
            P("expert", None, None),
        ),
        out_specs=(P(("dp", "expert"), None), P("expert", "dp", None), P("expert", "dp", None)),
        check_vma=False,
    )
```

```python
import jax
import jax.numpy as jnp
from jax import lax
from jax.experimental import pallas as pl
from jax.experimental.pallas import tpu as pltpu
from jax.sharding import PartitionSpec as P

SLOTS = 32
SIDE = 4
VMEM_LIMIT = 48 * 1024 * 1024


def slot_table(routed, num_experts):
    rows = routed.shape[0]
    places = jnp.arange(rows, dtype=jnp.int32)
    same = (routed[:, None] == routed[None, :]) & (places[:, None] < places[None, :])
    slots = jnp.sum(same.astype(jnp.int32), axis=0)
    target = routed * SLOTS + slots
    spots = jnp.arange(num_experts * SLOTS, dtype=jnp.int32)
    return (spots[:, None] == target[None, :]).astype(jnp.bfloat16)


def dgate_up_kernel(w_ref, dy_ref, a_ref, s_ref, out_ref):
    dhidden = lax.dot_general(
        w_ref[...], dy_ref[...], (((1,), (1,)), ((), ())), preferred_element_type=jnp.float32
    )
    out_ref[0] = (dhidden * a_ref[...]).astype(jnp.bfloat16)
    out_ref[1] = (dhidden * s_ref[...]).astype(jnp.bfloat16)


def make_dgate_up(w_out_t, rows_dy, slope, silu):
    ff, width = w_out_t.shape
    rows = rows_dy.shape[0]
    tile = 256
    return pl.pallas_call(
        dgate_up_kernel,
        grid=(ff // tile,),
        in_specs=[
            pl.BlockSpec((tile, width), lambda i: (i, 0)),
            pl.BlockSpec((rows, width), lambda i: (0, 0)),
            pl.BlockSpec((tile, rows), lambda i: (i, 0)),
            pl.BlockSpec((tile, rows), lambda i: (i, 0)),
        ],
        out_specs=pl.BlockSpec((2, tile, rows), lambda i: (0, i, 0)),
        out_shape=jax.ShapeDtypeStruct((2, ff, rows), jnp.bfloat16),
        compiler_params=pltpu.CompilerParams(vmem_limit_bytes=VMEM_LIMIT),
        cost_estimate=pl.CostEstimate(
            flops=2 * ff * rows * width, bytes_accessed=10 * ff * rows + 4 * rows * width, transcendentals=0
        ),
        name="dgate_up",
    )(w_out_t, rows_dy, slope, silu)


def drows_kernel(g_ref, w_ref, out_ref, turned):
    @pl.when(pl.program_id(0) == 0)
    def _():
        turned[...] = g_ref[...].T

    out_ref[...] = lax.dot_general(
        turned[...], w_ref[...], (((1,), (1,)), ((), ())), preferred_element_type=jnp.float32
    ).astype(jnp.bfloat16)


def make_drows(dgu_t, w_in):
    ff2, rows = dgu_t.shape
    width = w_in.shape[0]
    tile = 512
    return pl.pallas_call(
        drows_kernel,
        grid=(width // tile,),
        in_specs=[
            pl.BlockSpec((ff2, rows), lambda i: (0, 0)),
            pl.BlockSpec((tile, ff2), lambda i: (i, 0)),
        ],
        out_specs=pl.BlockSpec((rows, tile), lambda i: (0, i)),
        out_shape=jax.ShapeDtypeStruct((rows, width), jnp.bfloat16),
        scratch_shapes=[pltpu.VMEM((rows, ff2), jnp.bfloat16)],
        compiler_params=pltpu.CompilerParams(vmem_limit_bytes=VMEM_LIMIT),
        cost_estimate=pl.CostEstimate(
            flops=2 * ff2 * rows * width, bytes_accessed=2 * ff2 * (rows + width), transcendentals=0
        ),
        name="drows",
    )(dgu_t, w_in)


def partial_kernel(parts, table, *refs):
    out_ref = refs[-1]
    at = 0
    row = 0
    for start, count in parts:
        left = refs[at][start : start + count, :]
        right = jnp.concatenate([refs[at + 1 + i][...] for i in range(SIDE)], axis=1)
        out_ref[row : row + count, :] = jnp.dot(
            left, right, preferred_element_type=jnp.float32
        ).astype(jnp.bfloat16)
        at += 1 + SIDE
        row += count


def make_partial(table, pieces, name):
    blocks = table.shape[0]
    lane = 128
    specs, operands, parts = [], [], []
    for left, block, index, start, count, right in pieces:
        rows = left.shape[1]
        specs.append(pl.BlockSpec((block, rows), lambda i, t, index=index: (index, 0)))
        operands.append(left)
        for k in range(SIDE):
            specs.append(pl.BlockSpec((rows, lane), lambda i, t, k=k: (0, t[i * SIDE + k])))
            operands.append(right)
        parts.append((start, count))
    total = sum(count for _, count in parts)
    return pl.pallas_call(
        lambda table, *refs: partial_kernel(parts, table, *refs),
        grid_spec=pltpu.PrefetchScalarGridSpec(
            num_scalar_prefetch=1,
            grid=(blocks // SIDE,),
            in_specs=specs,
            out_specs=pl.BlockSpec((total, SIDE * lane), lambda i, t: (0, i)),
        ),
        out_shape=jax.ShapeDtypeStruct((total, blocks * lane), jnp.bfloat16),
        compiler_params=pltpu.CompilerParams(vmem_limit_bytes=VMEM_LIMIT),
        cost_estimate=pl.CostEstimate(
            flops=2 * total * rows * blocks * lane,
            bytes_accessed=2 * (total * rows + rows * blocks * lane + total * blocks * lane),
            transcendentals=0,
        ),
        name=name,
    )(table, *operands)


def pair_perm(axis, odd):
    def mate(i):
        return (3 - i) if odd else (i ^ 1)

    return [
        (x * SIDE + y, mate(x) * SIDE + y if axis == 0 else x * SIDE + mate(y))
        for x in range(SIDE)
        for y in range(SIDE)
    ]


FLOWS = ((0, False), (0, True), (1, False), (1, True))


def first_table(at, axis, odd):
    i = at[axis]
    minor = jnp.arange(SIDE, dtype=jnp.int32)

    def blocks(a, b):
        major = jnp.array([a, b], jnp.int32)
        ids = major[:, None] * SIDE + minor[None, :] if axis == 0 else minor[None, :] * SIDE + major[:, None]
        return ids.reshape(-1)

    low, high = (blocks(0, 1), blocks(2, 3)) if odd else (blocks(0, 3), blocks(1, 2))
    mine_low = (i < 2) if odd else ((i == 0) | (i == 3))
    return jnp.where(mine_low, high, low), jnp.where(mine_low, low, high)


def halves(block, at, axis, odd, step):
    i = at[axis]
    n = block.shape[1]
    if step % 2 == 1:
        low, high = block[:, : n // 2], block[:, n // 2 :]
        mine_low = (i % 2 == 0) if odd else (i < 2)
    else:
        q = n // 4
        if odd:
            low, high = block[:, : 2 * q], block[:, 2 * q :]
            mine_low = i < 2
        else:
            low = jnp.concatenate([block[:, :q], block[:, 3 * q :]], axis=1)
            high = block[:, q : 3 * q]
            mine_low = (i == 0) | (i == 3)
    return jnp.where(mine_low, high, low), jnp.where(mine_low, low, high)


def local(tokens, out_grads, expert_ids, w_gate_up, w_down_t):
    num_experts = lax.axis_size("expert")
    width = tokens.shape[1]
    ff = w_down_t.shape[2]
    rows = num_experts * SLOTS
    dispatch = slot_table(expert_ids[:, 0], num_experts)

    def send(values):
        slots = jnp.dot(dispatch, values, preferred_element_type=jnp.float32).astype(jnp.bfloat16)
        slots = slots.reshape(num_experts, SLOTS, width)
        got = lax.all_to_all(slots, "expert", split_axis=0, concat_axis=0, tiled=True)
        return got.reshape(rows, width)

    rows_x = send(tokens)
    rows_dy = send(out_grads)
    w_in = w_gate_up[0]
    w_out_t = w_down_t[0].T

    gate_up = lax.dot_general(
        w_in, rows_x, (((0,), (1,)), ((), ())), preferred_element_type=jnp.float32
    )
    gate = gate_up[:ff]
    upper = gate_up[ff:]
    sig = jax.nn.sigmoid(gate)
    silu = gate * sig
    hidden = (silu * upper).astype(jnp.bfloat16)
    slope = upper * sig * (1.0 + gate * (1.0 - sig))

    me = lax.axis_index("dp")
    at = (me // SIDE, me % SIDE)
    tables = [first_table(at, axis, odd) for axis, odd in FLOWS]

    dgu = make_dgate_up(w_out_t, rows_dy, slope, silu).reshape(2 * ff, rows)
    per = 3 * ff // 4
    left = 2 * ff - 2 * per
    pieces = (
        [(dgu, per, 0, 0, per, rows_x)],
        [(dgu, per, 1, 0, per, rows_x)],
        [(dgu, left, 2 * per // left, 0, left, rows_x), (hidden, per - left, 0, 0, per - left, rows_dy)],
        [(hidden, ff, 0, per - left, per, rows_dy)],
    )
    blocks = [None] * 4
    for f in (3, 0, 1, 2):
        axis, odd = FLOWS[f]
        give = make_partial(tables[f][0], pieces[f], "give")
        got = lax.ppermute(give, "dp", pair_perm(axis, odd))
        keep = make_partial(tables[f][1], pieces[f], "keep")
        blocks[f] = (keep.astype(jnp.float32) + got.astype(jnp.float32)).astype(jnp.bfloat16)

    drows = make_drows(dgu, w_in)
    returned = lax.all_to_all(
        drows.reshape(num_experts, SLOTS, width), "expert", split_axis=0, concat_axis=0, tiled=True
    ).reshape(rows, width)
    token_grads = lax.dot_general(
        dispatch, returned, (((0,), (0,)), ((), ())), preferred_element_type=jnp.float32
    ).astype(jnp.bfloat16)

    for step in range(1, 4):
        for f, (first_axis, first_odd) in enumerate(FLOWS):
            axis = first_axis if step < 2 else 1 - first_axis
            odd = first_odd if step % 2 == 0 else not first_odd
            give, keep = halves(blocks[f], at, axis, first_odd, step)
            got = lax.ppermute(give, "dp", pair_perm(axis, odd))
            blocks[f] = (keep.astype(jnp.float32) + got.astype(jnp.float32)).astype(jnp.bfloat16)
    summed = jnp.concatenate(blocks, axis=0).T
    return (token_grads, summed[None, :, : 2 * ff], summed[None, :, 2 * ff :])


def solution(mesh):
    return jax.shard_map(
        local,
        mesh=mesh,
        in_specs=(
            P(("dp", "expert"), None),
            P(("dp", "expert"), None),
            P(("dp", "expert"), None),
            P("expert", None, None),
            P("expert", None, None),
        ),
        out_specs=(P(("dp", "expert"), None), P("expert", "dp", None), P("expert", "dp", None)),
        check_vma=False,
    )
```

```python
import jax
import jax.numpy as jnp
from jax import lax
from jax.experimental import pallas as pl
from jax.experimental.pallas import tpu as pltpu
from jax.sharding import PartitionSpec as P

SLOTS = 32
SIDE = 4
LANE = 128
CHUNKS = 4


def slot_table(routed, num_experts):
    rows = routed.shape[0]
    places = jnp.arange(rows, dtype=jnp.int32)
    same = (routed[:, None] == routed[None, :]) & (places[:, None] < places[None, :])
    slots = jnp.sum(same.astype(jnp.int32), axis=0)
    target = routed * SLOTS + slots
    spots = jnp.arange(num_experts * SLOTS, dtype=jnp.int32)
    return (spots[:, None] == target[None, :]).astype(jnp.bfloat16)


def feature_blocks(ref, table, f, chunk):
    pair = [
        ref[:, pl.ds(pl.multiple_of(table[f, 2 * chunk + k] * LANE, LANE), LANE)] for k in range(2)
    ]
    return jnp.concatenate(pair, axis=1)


def product(left, right):
    return jnp.dot(left, right, preferred_element_type=jnp.float32).astype(jnp.bfloat16)


def dgate_up_kernel(table, w_ref, dy_ref, a_ref, s_ref, hid_ref, out_ref, give_ref):
    step = pl.program_id(0)
    last = pl.num_programs(0) - 1
    start = hid_ref.shape[0] - give_ref.shape[0]
    for chunk in range(CHUNKS):

        @pl.when(step == jnp.minimum(chunk, last))
        def _():
            give_ref[:, 2 * LANE * chunk : 2 * LANE * (chunk + 1)] = product(
                hid_ref[start:, :], feature_blocks(dy_ref, table, 3, chunk)
            )

    dhidden = lax.dot_general(
        w_ref[...], dy_ref[...], (((1,), (1,)), ((), ())), preferred_element_type=jnp.float32
    )
    out_ref[0] = (dhidden * a_ref[...]).astype(jnp.bfloat16)
    out_ref[1] = (dhidden * s_ref[...]).astype(jnp.bfloat16)


def make_dgate_up(table, w_out_t, rows_dy, slope, silu, hidden):
    ff, width = w_out_t.shape
    rows = rows_dy.shape[0]
    tile = 256
    per = 3 * ff // 4
    return pl.pallas_call(
        dgate_up_kernel,
        grid_spec=pltpu.PrefetchScalarGridSpec(
            num_scalar_prefetch=1,
            grid=(ff // tile,),
            in_specs=[
                pl.BlockSpec((tile, width), lambda i, t: (i, 0)),
                pl.BlockSpec((rows, width), lambda i, t: (0, 0)),
                pl.BlockSpec((tile, rows), lambda i, t: (i, 0)),
                pl.BlockSpec((tile, rows), lambda i, t: (i, 0)),
                pl.BlockSpec((ff, rows), lambda i, t: (0, 0)),
            ],
            out_specs=[
                pl.BlockSpec((2, tile, rows), lambda i, t: (0, i, 0)),
                pl.BlockSpec((per, 2 * CHUNKS * LANE), lambda i, t: (0, 0)),
            ],
        ),
        out_shape=[
            jax.ShapeDtypeStruct((2, ff, rows), jnp.bfloat16),
            jax.ShapeDtypeStruct((per, 2 * CHUNKS * LANE), jnp.bfloat16),
        ],
        compiler_params=pltpu.CompilerParams(vmem_limit_bytes=24 * 1024 * 1024),
        cost_estimate=pl.CostEstimate(
            flops=2 * ff * rows * width + 4 * per * rows * CHUNKS * LANE,
            bytes_accessed=12 * ff * rows + 4 * rows * width + 4 * per * CHUNKS * LANE,
            transcendentals=0,
        ),
        name="dgate_up",
    )(table, w_out_t, rows_dy, slope, silu, hidden)


def partials_kernel(flows, table, dgu_ref, hid_ref, x_ref, dy_ref, *outs):
    per = outs[0].shape[0]
    split = dgu_ref.shape[0]
    for out, f in zip(outs, flows):
        low, high = f * per, (f + 1) * per
        for chunk in range(CHUNKS):
            to = slice(2 * LANE * chunk, 2 * LANE * (chunk + 1))
            if low < split:
                end = min(high, split)
                out[: end - low, to] = product(dgu_ref[low:end, :], feature_blocks(x_ref, table, f, chunk))
            if high > split:
                begin = max(low, split)
                out[begin - low :, to] = product(
                    hid_ref[begin - split : high - split, :], feature_blocks(dy_ref, table, f, chunk)
                )


def make_partials(flows, table, dgu, hidden, rows_x, rows_dy, name):
    rows = rows_x.shape[0]
    per = (dgu.shape[0] + hidden.shape[0]) // 4
    size = (per, 2 * CHUNKS * LANE)
    whole = pl.BlockSpec(memory_space=pltpu.VMEM)
    return pl.pallas_call(
        lambda *refs: partials_kernel(flows, *refs),
        in_specs=[pl.BlockSpec(memory_space=pltpu.SMEM)] + [whole] * 4,
        out_specs=[whole] * len(flows),
        out_shape=[jax.ShapeDtypeStruct(size, jnp.bfloat16)] * len(flows),
        compiler_params=pltpu.CompilerParams(vmem_limit_bytes=24 * 1024 * 1024),
        cost_estimate=pl.CostEstimate(
            flops=2 * len(flows) * per * rows * size[1],
            bytes_accessed=2 * (dgu.size + hidden.size + 2 * rows_x.size + len(flows) * per * size[1]),
            transcendentals=0,
        ),
        name=name,
    )(table, dgu, hidden, rows_x, rows_dy)


def pair_perm(axis, odd):
    def mate(i):
        return (3 - i) if odd else (i ^ 1)

    return [
        (x * SIDE + y, mate(x) * SIDE + y if axis == 0 else x * SIDE + mate(y))
        for x in range(SIDE)
        for y in range(SIDE)
    ]


FLOWS = ((0, False), (0, True), (1, False), (1, True))


def first_table(at, axis, odd):
    i = at[axis]
    minor = jnp.arange(SIDE, dtype=jnp.int32)

    def blocks(a, b):
        major = jnp.array([a, b], jnp.int32)
        ids = major[:, None] * SIDE + minor[None, :] if axis == 0 else minor[None, :] * SIDE + major[:, None]
        return ids.reshape(-1)

    low, high = (blocks(0, 1), blocks(2, 3)) if odd else (blocks(0, 3), blocks(1, 2))
    mine_low = (i < 2) if odd else ((i == 0) | (i == 3))
    return jnp.where(mine_low, high, low), jnp.where(mine_low, low, high)


def halves(block, at, axis, odd, step):
    i = at[axis]
    n = block.shape[1]
    if step % 2 == 1:
        low, high = block[:, : n // 2], block[:, n // 2 :]
        mine_low = (i % 2 == 0) if odd else (i < 2)
    else:
        q = n // 4
        if odd:
            low, high = block[:, : 2 * q], block[:, 2 * q :]
            mine_low = i < 2
        else:
            low = jnp.concatenate([block[:, :q], block[:, 3 * q :]], axis=1)
            high = block[:, q : 3 * q]
            mine_low = (i == 0) | (i == 3)
    return jnp.where(mine_low, high, low), jnp.where(mine_low, low, high)


def local(tokens, out_grads, expert_ids, w_gate_up, w_down_t):
    num_experts = lax.axis_size("expert")
    width = tokens.shape[1]
    ff = w_down_t.shape[2]
    rows = num_experts * SLOTS
    dispatch = slot_table(expert_ids[:, 0], num_experts)

    def send(values):
        slots = jnp.dot(dispatch, values, preferred_element_type=jnp.float32).astype(jnp.bfloat16)
        slots = slots.reshape(num_experts, SLOTS, width)
        got = lax.all_to_all(slots, "expert", split_axis=0, concat_axis=0, tiled=True)
        return got.reshape(rows, width)

    rows_x = send(tokens)
    rows_dy = send(out_grads)
    w_in = w_gate_up[0]
    w_out_t = w_down_t[0].T

    gate_up = lax.dot_general(
        w_in, rows_x, (((0,), (1,)), ((), ())), preferred_element_type=jnp.float32
    )
    gate = gate_up[:ff]
    upper = gate_up[ff:]
    sig = jax.nn.sigmoid(gate)
    silu = gate * sig
    hidden = (silu * upper).astype(jnp.bfloat16)
    slope = upper * sig * (1.0 + gate * (1.0 - sig))

    me = lax.axis_index("dp")
    at = (me // SIDE, me % SIDE)
    tables = [first_table(at, axis, odd) for axis, odd in FLOWS]

    to_give = jnp.stack([t[0] for t in tables])
    to_keep = jnp.stack([t[1] for t in tables])
    dgu, last_give = make_dgate_up(to_give, w_out_t, rows_dy, slope, silu, hidden)
    dgu = dgu.reshape(2 * ff, rows)
    gives = [*make_partials((0, 1, 2), to_give, dgu, hidden, rows_x, rows_dy, "give"), last_give]
    gots = [None] * 4
    for f in (3, 0, 1, 2):
        gots[f] = lax.ppermute(gives[f], "dp", pair_perm(*FLOWS[f]))
    drows = lax.dot_general(
        dgu, w_in, (((0,), (1,)), ((), ())), preferred_element_type=jnp.float32
    ).astype(jnp.bfloat16)
    keeps = make_partials((0, 1, 2, 3), to_keep, dgu, hidden, rows_x, rows_dy, "keep")
    blocks = [
        (keep.astype(jnp.float32) + got.astype(jnp.float32)).astype(jnp.bfloat16)
        for keep, got in zip(keeps, gots)
    ]

    returned = lax.all_to_all(
        drows.reshape(num_experts, SLOTS, width), "expert", split_axis=0, concat_axis=0, tiled=True
    ).reshape(rows, width)
    token_grads = lax.dot_general(
        dispatch, returned, (((0,), (0,)), ((), ())), preferred_element_type=jnp.float32
    ).astype(jnp.bfloat16)

    for step in range(1, 4):
        for f, (first_axis, first_odd) in enumerate(FLOWS):
            axis = first_axis if step < 2 else 1 - first_axis
            odd = first_odd if step % 2 == 0 else not first_odd
            give, keep = halves(blocks[f], at, axis, first_odd, step)
            got = lax.ppermute(give, "dp", pair_perm(axis, odd))
            blocks[f] = (keep.astype(jnp.float32) + got.astype(jnp.float32)).astype(jnp.bfloat16)
    summed = jnp.concatenate(blocks, axis=0).T
    return (token_grads, summed[None, :, : 2 * ff], summed[None, :, 2 * ff :])


def solution(mesh):
    return jax.shard_map(
        local,
        mesh=mesh,
        in_specs=(
            P(("dp", "expert"), None),
            P(("dp", "expert"), None),
            P(("dp", "expert"), None),
            P("expert", None, None),
            P("expert", None, None),
        ),
        out_specs=(P(("dp", "expert"), None), P("expert", "dp", None), P("expert", "dp", None)),
        check_vma=False,
    )
```

```python
import jax
import jax.numpy as jnp
from jax import lax
from jax.experimental import pallas as pl
from jax.experimental.pallas import tpu as pltpu
from jax.sharding import PartitionSpec as P

SLOTS = 32
SIDE = 4
LANE = 128
CHUNKS = 4
SMALL = pl.CostEstimate(flops=1000000, bytes_accessed=100000, transcendentals=0)


def token_slots(routed):
    rows = routed.shape[0]
    places = jnp.arange(rows, dtype=jnp.int32)
    same = (routed[:, None] == routed[None, :]) & (places[:, None] < places[None, :])
    return jnp.sum(same.astype(jnp.int32), axis=0)


def one_hot_rows(target, count):
    spots = jnp.arange(count, dtype=jnp.int32)
    return (spots[:, None] == target[None, :]).astype(jnp.bfloat16)


def feature_blocks(ref, table, f, chunk):
    pair = [
        ref[:, pl.ds(pl.multiple_of(table[f, 2 * chunk + k] * LANE, LANE), LANE)] for k in range(2)
    ]
    return jnp.concatenate(pair, axis=1)


def product(left, right):
    return jnp.dot(left, right, preferred_element_type=jnp.float32).astype(jnp.bfloat16)


def join_copies(places, pieces, to_ref, sems):
    copies = []
    for d, piece in enumerate(pieces):
        for k in range(2):
            row = pl.multiple_of(places[2 * d + k] * SLOTS, SLOTS)
            copies.append(
                pltpu.make_async_copy(piece.at[k], to_ref.at[pl.ds(row, SLOTS)], sems.at[2 * d + k])
            )
    return copies


def join_kernel(places, *refs):
    *pieces, out_ref, sems = refs
    copies = join_copies(places, pieces, out_ref, sems)
    for copy in copies:
        copy.start()
    for copy in copies:
        copy.wait()


def join(places, pieces):
    width = pieces[0].shape[2]
    rows = 2 * len(pieces) * SLOTS
    return pl.pallas_call(
        join_kernel,
        in_specs=[pl.BlockSpec(memory_space=pltpu.SMEM)] + [pl.BlockSpec(memory_space=pl.ANY)] * len(pieces),
        out_specs=pl.BlockSpec(memory_space=pltpu.VMEM),
        out_shape=jax.ShapeDtypeStruct((rows, width), jnp.bfloat16),
        scratch_shapes=[pltpu.SemaphoreType.DMA((2 * len(pieces),))],
        compiler_params=pltpu.CompilerParams(vmem_limit_bytes=16 * 1024 * 1024),
        cost_estimate=SMALL,
        name="join",
    )(places, *pieces)


def dgate_up_kernel(places, table, w_ref, a_ref, s_ref, hid_ref, *refs):
    *pieces, dy_ref, out_ref, give_ref, sems = refs
    copies = join_copies(places, pieces, dy_ref, sems)
    for copy in copies:
        copy.start()
    for copy in copies:
        copy.wait()
    start = hid_ref.shape[0] - give_ref.shape[0]
    for chunk in range(CHUNKS):
        give_ref[:, 2 * LANE * chunk : 2 * LANE * (chunk + 1)] = product(
            hid_ref[start:, :], feature_blocks(dy_ref, table, 3, chunk)
        )
    tile = 256
    for low in range(0, w_ref.shape[0], tile):
        part = slice(low, low + tile)
        dhidden = lax.dot_general(
            w_ref[part, :], dy_ref[...], (((1,), (1,)), ((), ())), preferred_element_type=jnp.float32
        )
        out_ref[0, part] = (dhidden * a_ref[part, :]).astype(jnp.bfloat16)
        out_ref[1, part] = (dhidden * s_ref[part, :]).astype(jnp.bfloat16)


def make_dgate_up(places, table, w_out_t, slope, silu, hidden, pieces):
    ff, width = w_out_t.shape
    rows = 2 * len(pieces) * SLOTS
    per = 3 * ff // 4
    whole = pl.BlockSpec(memory_space=pltpu.VMEM)
    small = pl.BlockSpec(memory_space=pltpu.SMEM)
    return pl.pallas_call(
        dgate_up_kernel,
        in_specs=[small] * 2 + [whole] * 4 + [pl.BlockSpec(memory_space=pl.ANY)] * len(pieces),
        out_specs=[whole] * 3,
        out_shape=[
            jax.ShapeDtypeStruct((rows, width), jnp.bfloat16),
            jax.ShapeDtypeStruct((2, ff, rows), jnp.bfloat16),
            jax.ShapeDtypeStruct((per, 2 * CHUNKS * LANE), jnp.bfloat16),
        ],
        scratch_shapes=[pltpu.SemaphoreType.DMA((2 * len(pieces),))],
        compiler_params=pltpu.CompilerParams(vmem_limit_bytes=24 * 1024 * 1024),
        cost_estimate=SMALL,
        name="dgate_up",
    )(places, table, w_out_t, slope, silu, hidden, *pieces)


def partials_kernel(flows, table, dgu_ref, hid_ref, x_ref, dy_ref, *outs):
    per = outs[0].shape[0]
    split = dgu_ref.shape[0]
    for out, f in zip(outs, flows):
        low, high = f * per, (f + 1) * per
        for chunk in range(CHUNKS):
            to = slice(2 * LANE * chunk, 2 * LANE * (chunk + 1))
            if low < split:
                end = min(high, split)
                out[: end - low, to] = product(dgu_ref[low:end, :], feature_blocks(x_ref, table, f, chunk))
            if high > split:
                begin = max(low, split)
                out[begin - low :, to] = product(
                    hid_ref[begin - split : high - split, :], feature_blocks(dy_ref, table, f, chunk)
                )


def make_partials(flows, table, dgu, hidden, rows_x, rows_dy, name):
    rows = rows_x.shape[0]
    per = (dgu.shape[0] + hidden.shape[0]) // 4
    size = (per, 2 * CHUNKS * LANE)
    whole = pl.BlockSpec(memory_space=pltpu.VMEM)
    return pl.pallas_call(
        lambda *refs: partials_kernel(flows, *refs),
        in_specs=[pl.BlockSpec(memory_space=pltpu.SMEM)] + [whole] * 4,
        out_specs=[whole] * len(flows),
        out_shape=[jax.ShapeDtypeStruct(size, jnp.bfloat16)] * len(flows),
        compiler_params=pltpu.CompilerParams(vmem_limit_bytes=24 * 1024 * 1024),
        cost_estimate=SMALL,
        name=name,
    )(table, dgu, hidden, rows_x, rows_dy)


def pair_perm(axis, odd):
    def mate(i):
        return (3 - i) if odd else (i ^ 1)

    return [
        (x * SIDE + y, mate(x) * SIDE + y if axis == 0 else x * SIDE + mate(y))
        for x in range(SIDE)
        for y in range(SIDE)
    ]


FLOWS = ((0, False), (0, True), (1, False), (1, True))


def first_table(at, axis, odd):
    i = at[axis]
    minor = jnp.arange(SIDE, dtype=jnp.int32)

    def blocks(a, b):
        major = jnp.array([a, b], jnp.int32)
        ids = major[:, None] * SIDE + minor[None, :] if axis == 0 else minor[None, :] * SIDE + major[:, None]
        return ids.reshape(-1)

    low, high = (blocks(0, 1), blocks(2, 3)) if odd else (blocks(0, 3), blocks(1, 2))
    mine_low = (i < 2) if odd else ((i == 0) | (i == 3))
    return jnp.where(mine_low, high, low), jnp.where(mine_low, low, high)


def halves(block, at, axis, odd, step):
    i = at[axis]
    n = block.shape[1]
    if step % 2 == 1:
        low, high = block[:, : n // 2], block[:, n // 2 :]
        mine_low = (i % 2 == 0) if odd else (i < 2)
    else:
        q = n // 4
        if odd:
            low, high = block[:, : 2 * q], block[:, 2 * q :]
            mine_low = i < 2
        else:
            low = jnp.concatenate([block[:, :q], block[:, 3 * q :]], axis=1)
            high = block[:, q : 3 * q]
            mine_low = (i == 0) | (i == 3)
    return jnp.where(mine_low, high, low), jnp.where(mine_low, low, high)


def local(tokens, out_grads, expert_ids, w_gate_up, w_down_t):
    num_experts = lax.axis_size("expert")
    chips = num_experts // 2
    width = tokens.shape[1]
    ff = w_down_t.shape[2]
    rows = num_experts * SLOTS
    place = lax.axis_index("expert")
    chip, core = place // 2, place % 2
    routed = expert_ids[:, 0]
    slots = token_slots(routed)
    relative = ((routed // 2 - chip + chips) % chips) * SLOTS + slots
    own = routed % 2 == core
    mine_rows = one_hot_rows(jnp.where(own, relative, -1), chips * SLOTS)
    other_rows = one_hot_rows(jnp.where(own, -1, relative), chips * SLOTS)
    distance = jnp.arange(chips, dtype=jnp.int32)
    places = (
        ((chip - distance + chips) % chips)[:, None] * 2
        + jnp.array([0, 1], jnp.int32)[None, :] * (1 - 2 * core)
        + core
    ).reshape(-1)

    def send(values):
        def pack(table):
            packed = jnp.dot(table, values, preferred_element_type=jnp.float32)
            return packed.astype(jnp.bfloat16).reshape(chips, SLOTS, width)

        other = lax.ppermute(pack(other_rows), "expert", [(i, i ^ 1) for i in range(num_experts)])
        both = jnp.stack([pack(mine_rows), other], axis=1)
        pieces = [both[0]] + [None] * (chips - 1)
        for d in (4, 3, 5, 2, 6, 1, 7):
            pieces[d] = lax.ppermute(
                both[d], "expert", [(i, (i + 2 * d) % num_experts) for i in range(num_experts)]
            )
        return pieces

    rows_x = join(places, send(tokens))
    pieces_dy = send(out_grads)
    w_in = w_gate_up[0]
    w_out_t = w_down_t[0].T

    gate_up = lax.dot_general(
        w_in, rows_x, (((0,), (1,)), ((), ())), preferred_element_type=jnp.float32
    )
    gate = gate_up[:ff]
    upper = gate_up[ff:]
    sig = jax.nn.sigmoid(gate)
    silu = gate * sig
    hidden = (silu * upper).astype(jnp.bfloat16)
    slope = upper * sig * (1.0 + gate * (1.0 - sig))

    me = lax.axis_index("dp")
    at = (me // SIDE, me % SIDE)
    tables = [first_table(at, axis, odd) for axis, odd in FLOWS]

    to_give = jnp.stack([t[0] for t in tables])
    to_keep = jnp.stack([t[1] for t in tables])
    rows_dy, dgu, last_give = make_dgate_up(places, to_give, w_out_t, slope, silu, hidden, pieces_dy)
    dgu = dgu.reshape(2 * ff, rows)
    gives = [*make_partials((0, 1, 2), to_give, dgu, hidden, rows_x, rows_dy, "give"), last_give]
    gots = [None] * 4
    for f in (3, 0, 1, 2):
        gots[f] = lax.ppermute(gives[f], "dp", pair_perm(*FLOWS[f]))
    drows = lax.dot_general(
        dgu, w_in, (((0,), (1,)), ((), ())), preferred_element_type=jnp.float32
    ).astype(jnp.bfloat16)
    keeps = make_partials((0, 1, 2, 3), to_keep, dgu, hidden, rows_x, rows_dy, "keep")
    blocks = [
        (keep.astype(jnp.float32) + got.astype(jnp.float32)).astype(jnp.bfloat16)
        for keep, got in zip(keeps, gots)
    ]

    returned = lax.all_to_all(
        drows.reshape(num_experts, SLOTS, width), "expert", split_axis=0, concat_axis=0, tiled=True
    ).reshape(rows, width)
    token_grads = lax.dot_general(
        one_hot_rows(routed * SLOTS + slots, rows), returned, (((0,), (0,)), ((), ())), preferred_element_type=jnp.float32
    ).astype(jnp.bfloat16)

    for step in range(1, 4):
        for f, (first_axis, first_odd) in enumerate(FLOWS):
            axis = first_axis if step < 2 else 1 - first_axis
            odd = first_odd if step % 2 == 0 else not first_odd
            give, keep = halves(blocks[f], at, axis, first_odd, step)
            got = lax.ppermute(give, "dp", pair_perm(axis, odd))
            blocks[f] = (keep.astype(jnp.float32) + got.astype(jnp.float32)).astype(jnp.bfloat16)
    summed = jnp.concatenate(blocks, axis=0).T
    return (token_grads, summed[None, :, : 2 * ff], summed[None, :, 2 * ff :])


def solution(mesh):
    return jax.shard_map(
        local,
        mesh=mesh,
        in_specs=(
            P(("dp", "expert"), None),
            P(("dp", "expert"), None),
            P(("dp", "expert"), None),
            P("expert", None, None),
            P("expert", None, None),
        ),
        out_specs=(P(("dp", "expert"), None), P("expert", "dp", None), P("expert", "dp", None)),
        check_vma=False,
    )
```

```python
import jax
import jax.numpy as jnp
from jax import lax
from jax.experimental import pallas as pl
from jax.experimental.pallas import tpu as pltpu
from jax.sharding import PartitionSpec as P

SLOTS = 32
SIDE = 4
LANE = 128
CHUNKS = 4
SMALL = pl.CostEstimate(flops=1000000, bytes_accessed=100000, transcendentals=0)


def token_slots(routed):
    rows = routed.shape[0]
    places = jnp.arange(rows, dtype=jnp.int32)
    same = (routed[:, None] == routed[None, :]) & (places[:, None] < places[None, :])
    return jnp.sum(same.astype(jnp.int32), axis=0)


def one_hot_rows(target, count):
    spots = jnp.arange(count, dtype=jnp.int32)
    return (spots[:, None] == target[None, :]).astype(jnp.bfloat16)


def feature_blocks(ref, table, f, chunk):
    pair = [
        ref[:, pl.ds(pl.multiple_of(table[f, 2 * chunk + k] * LANE, LANE), LANE)] for k in range(2)
    ]
    return jnp.concatenate(pair, axis=1)


def lanes(chunk):
    return pl.ds(pl.multiple_of(chunk * (2 * LANE), 2 * LANE), 2 * LANE)


def dot32(left, right):
    return jnp.dot(left, right, preferred_element_type=jnp.float32)


def product(left, right):
    return dot32(left, right).astype(jnp.bfloat16)


def flow_parts(f, per, split):
    low, high = f * per, (f + 1) * per
    parts = []
    if low < split:
        parts.append((True, low, min(high, split) - low, 0))
    if high > split:
        begin = max(low, split)
        parts.append((False, begin - split, high - begin, begin - low))
    return parts


def join_copies(places, pieces, to_ref, sems):
    copies = []
    for d, piece in enumerate(pieces):
        for k in range(2):
            row = pl.multiple_of(places[2 * d + k] * SLOTS, SLOTS)
            copies.append(
                pltpu.make_async_copy(piece.at[k], to_ref.at[pl.ds(row, SLOTS)], sems.at[2 * d + k])
            )
    return copies


def join_kernel(places, *refs):
    *pieces, out_ref, sems = refs
    copies = join_copies(places, pieces, out_ref, sems)
    for copy in copies:
        copy.start()
    for copy in copies:
        copy.wait()


def join(places, pieces):
    width = pieces[0].shape[2]
    rows = 2 * len(pieces) * SLOTS
    return pl.pallas_call(
        join_kernel,
        in_specs=[pl.BlockSpec(memory_space=pltpu.SMEM)] + [pl.BlockSpec(memory_space=pl.ANY)] * len(pieces),
        out_specs=pl.BlockSpec(memory_space=pltpu.VMEM),
        out_shape=jax.ShapeDtypeStruct((rows, width), jnp.bfloat16),
        scratch_shapes=[pltpu.SemaphoreType.DMA((2 * len(pieces),))],
        compiler_params=pltpu.CompilerParams(vmem_limit_bytes=16 * 1024 * 1024),
        cost_estimate=SMALL,
        name="join",
    )(places, *pieces)


def dgate_up_kernel(places, table, w_ref, a_ref, s_ref, hid_ref, *refs):
    *pieces, dy_ref, out_ref, give_ref, sems = refs
    copies = join_copies(places, pieces, dy_ref, sems)
    for copy in copies:
        copy.start()
    for copy in copies:
        copy.wait()
    start = hid_ref.shape[0] - give_ref.shape[0]

    def give(chunk, carry):
        give_ref[:, lanes(chunk)] = product(hid_ref[start:, :], feature_blocks(dy_ref, table, 3, chunk))
        return carry

    lax.fori_loop(0, CHUNKS, give, 0)
    tile = 256

    def dhidden_tile(i, carry):
        part = pl.ds(pl.multiple_of(i * tile, tile), tile)
        dhidden = lax.dot_general(
            w_ref[part, :], dy_ref[...], (((1,), (1,)), ((), ())), preferred_element_type=jnp.float32
        )
        out_ref[0, part] = (dhidden * a_ref[part, :]).astype(jnp.bfloat16)
        out_ref[1, part] = (dhidden * s_ref[part, :]).astype(jnp.bfloat16)
        return carry

    lax.fori_loop(0, w_ref.shape[0] // tile, dhidden_tile, 0)


def make_dgate_up(places, table, w_out_t, slope, silu, hidden, pieces):
    ff, width = w_out_t.shape
    rows = 2 * len(pieces) * SLOTS
    per = 3 * ff // 4
    whole = pl.BlockSpec(memory_space=pltpu.VMEM)
    small = pl.BlockSpec(memory_space=pltpu.SMEM)
    return pl.pallas_call(
        dgate_up_kernel,
        in_specs=[small] * 2 + [whole] * 4 + [pl.BlockSpec(memory_space=pl.ANY)] * len(pieces),
        out_specs=[whole] * 3,
        out_shape=[
            jax.ShapeDtypeStruct((rows, width), jnp.bfloat16),
            jax.ShapeDtypeStruct((2, ff, rows), jnp.bfloat16),
            jax.ShapeDtypeStruct((per, 2 * CHUNKS * LANE), jnp.bfloat16),
        ],
        scratch_shapes=[pltpu.SemaphoreType.DMA((2 * len(pieces),))],
        compiler_params=pltpu.CompilerParams(vmem_limit_bytes=24 * 1024 * 1024),
        cost_estimate=SMALL,
        name="dgate_up",
    )(places, table, w_out_t, slope, silu, hidden, *pieces)


def gives_kernel(flows, table, dgu_ref, hid_ref, x_ref, dy_ref, *refs):
    n = len(flows)
    outs, stages, sems = refs[:n], refs[n : 2 * n], refs[2 * n]
    per = outs[0].shape[0]

    def copy(i, chunk):
        return pltpu.make_async_copy(
            stages[i].at[:, lanes(chunk)], outs[i].at[:, lanes(chunk)], sems.at[i, chunk]
        )

    for i, f in enumerate(flows):

        def body(chunk, carry):
            for from_dgu, first, count, row in flow_parts(f, per, dgu_ref.shape[0]):
                left, right = (dgu_ref, x_ref) if from_dgu else (hid_ref, dy_ref)
                stages[i][row : row + count, lanes(chunk)] = product(
                    left[first : first + count, :], feature_blocks(right, table, f, chunk)
                )
            copy(i, chunk).start()
            return carry

        lax.fori_loop(0, CHUNKS, body, 0)
    for i in range(n):
        for chunk in range(CHUNKS):
            copy(i, chunk).wait()


def make_gives(flows, table, dgu, hidden, rows_x, rows_dy):
    per = (dgu.shape[0] + hidden.shape[0]) // 4
    size = (per, 2 * CHUNKS * LANE)
    whole = pl.BlockSpec(memory_space=pltpu.VMEM)
    return pl.pallas_call(
        lambda *refs: gives_kernel(flows, *refs),
        in_specs=[pl.BlockSpec(memory_space=pltpu.SMEM)] + [whole] * 4,
        out_specs=[pl.BlockSpec(memory_space=pl.ANY)] * len(flows),
        out_shape=[jax.ShapeDtypeStruct(size, jnp.bfloat16)] * len(flows),
        scratch_shapes=[pltpu.VMEM(size, jnp.bfloat16)] * len(flows)
        + [pltpu.SemaphoreType.DMA((len(flows), CHUNKS))],
        compiler_params=pltpu.CompilerParams(vmem_limit_bytes=16 * 1024 * 1024),
        cost_estimate=SMALL,
        name="give",
    )(table, dgu, hidden, rows_x, rows_dy)


def merge_kernel(f, table, got_ref, *refs):
    *sides, give_ref, keep_ref = refs
    per = give_ref.shape[0]
    half = CHUNKS // 2
    for out, base in ((give_ref, 0), (keep_ref, half)):

        def body(i, carry):
            chunk = base + i
            for k, (_, first, count, row) in enumerate(flow_parts(f, per, 8 * per // 3)):
                total = dot32(
                    sides[2 * k][first : first + count, :], feature_blocks(sides[2 * k + 1], table, f, chunk)
                )
                total += got_ref[row : row + count, lanes(chunk)].astype(jnp.float32)
                out[row : row + count, lanes(i)] = total.astype(jnp.bfloat16)
            return carry

        lax.fori_loop(0, half, body, 0)


def merge(f, table, got, dgu, hidden, rows_x, rows_dy):
    per = got.shape[0]
    sides = []
    for from_dgu, *_ in flow_parts(f, per, dgu.shape[0]):
        sides += [dgu, rows_x] if from_dgu else [hidden, rows_dy]
    whole = pl.BlockSpec(memory_space=pltpu.VMEM)
    return pl.pallas_call(
        lambda *refs: merge_kernel(f, *refs),
        in_specs=[pl.BlockSpec(memory_space=pltpu.SMEM)] + [whole] * (1 + len(sides)),
        out_specs=[whole] * 2,
        out_shape=[jax.ShapeDtypeStruct((per, CHUNKS * LANE), jnp.bfloat16)] * 2,
        compiler_params=pltpu.CompilerParams(vmem_limit_bytes=12 * 1024 * 1024),
        cost_estimate=SMALL,
        name="merge",
    )(table, got, *sides)


def finish_kernel(*refs):
    *parts, up_ref, down_ref = refs
    n = len(parts) // 2
    total = jnp.concatenate(
        [parts[i][...].astype(jnp.float32) + parts[n + i][...].astype(jnp.float32) for i in range(n)], axis=0
    )
    split = up_ref.shape[1]
    up_ref[...] = total[:split].T.astype(jnp.bfloat16)
    down_ref[...] = total[split:].T.astype(jnp.bfloat16)


def finish(keeps, gots):
    per, lane = keeps[0].shape
    whole = pl.BlockSpec(memory_space=pltpu.VMEM)
    return pl.pallas_call(
        finish_kernel,
        in_specs=[whole] * 8,
        out_specs=[whole] * 2,
        out_shape=[
            jax.ShapeDtypeStruct((lane, 8 * per // 3), jnp.bfloat16),
            jax.ShapeDtypeStruct((lane, 4 * per // 3), jnp.bfloat16),
        ],
        compiler_params=pltpu.CompilerParams(vmem_limit_bytes=12 * 1024 * 1024),
        cost_estimate=SMALL,
        name="finish",
    )(*keeps, *gots)


def mate(i, odd):
    return (3 - i) if odd else (i ^ 1)


def pair_perm(axis, odd):
    return [
        (x * SIDE + y, mate(x, odd) * SIDE + y if axis == 0 else x * SIDE + mate(y, odd))
        for x in range(SIDE)
        for y in range(SIDE)
    ]


FLOWS = ((0, False), (0, True), (1, False), (1, True))


def first_table(at, axis, odd):
    a, b = at[axis], at[1 - axis]

    def kept(i):
        return [mate(i, not odd), i]

    minor = jnp.stack(kept(mate(b, odd)) + kept(b)).astype(jnp.int32)

    def blocks(i):
        major = jnp.stack(kept(i)).astype(jnp.int32)
        ids = major[:, None] * SIDE + minor[None, :] if axis == 0 else minor[None, :] * SIDE + major[:, None]
        return ids.reshape(-1)

    return blocks(mate(a, odd)), blocks(a)


def local(tokens, out_grads, expert_ids, w_gate_up, w_down_t):
    num_experts = lax.axis_size("expert")
    chips = num_experts // 2
    width = tokens.shape[1]
    ff = w_down_t.shape[2]
    rows = num_experts * SLOTS
    place = lax.axis_index("expert")
    chip, core = place // 2, place % 2
    routed = expert_ids[:, 0]
    slots = token_slots(routed)
    relative = ((routed // 2 - chip + chips) % chips) * SLOTS + slots
    own = routed % 2 == core
    mine_rows = one_hot_rows(jnp.where(own, relative, -1), chips * SLOTS)
    other_rows = one_hot_rows(jnp.where(own, -1, relative), chips * SLOTS)
    distance = jnp.arange(chips, dtype=jnp.int32)
    places = (
        ((chip - distance + chips) % chips)[:, None] * 2
        + jnp.array([0, 1], jnp.int32)[None, :] * (1 - 2 * core)
        + core
    ).reshape(-1)

    def send(values):
        def pack(table):
            packed = jnp.dot(table, values, preferred_element_type=jnp.float32)
            return packed.astype(jnp.bfloat16).reshape(chips, SLOTS, width)

        other = lax.ppermute(pack(other_rows), "expert", [(i, i ^ 1) for i in range(num_experts)])
        both = jnp.stack([pack(mine_rows), other], axis=1)
        pieces = [both[0]] + [None] * (chips - 1)
        for d in (4, 3, 5, 2, 6, 1, 7):
            pieces[d] = lax.ppermute(
                both[d], "expert", [(i, (i + 2 * d) % num_experts) for i in range(num_experts)]
            )
        return pieces

    rows_x = join(places, send(tokens))
    pieces_dy = send(out_grads)
    w_in = w_gate_up[0]
    w_out, rows_x = lax.optimization_barrier((w_down_t[0], rows_x))
    w_out_t = w_out.T

    gate_up = lax.dot_general(
        w_in, rows_x, (((0,), (1,)), ((), ())), preferred_element_type=jnp.float32
    )
    gate = gate_up[:ff]
    upper = gate_up[ff:]
    sig = jax.nn.sigmoid(gate)
    silu = gate * sig
    hidden = (silu * upper).astype(jnp.bfloat16)
    slope = upper * sig * (1.0 + gate * (1.0 - sig))

    me = lax.axis_index("dp")
    at = (me // SIDE, me % SIDE)
    tables = [first_table(at, axis, odd) for axis, odd in FLOWS]

    to_give = jnp.stack([t[0] for t in tables])
    to_keep = jnp.stack([t[1] for t in tables])
    rows_dy, dgu, last_give = make_dgate_up(places, to_give, w_out_t, slope, silu, hidden, pieces_dy)
    dgu = dgu.reshape(2 * ff, rows)
    gives = [*make_gives((0, 1, 2), to_give, dgu, hidden, rows_x, rows_dy), last_give]
    gots = [None] * 4
    for f in (3, 0, 1, 2):
        gots[f] = lax.ppermute(gives[f], "dp", pair_perm(*FLOWS[f]))
    drows = lax.dot_general(
        dgu, w_in, (((0,), (1,)), ((), ())), preferred_element_type=jnp.float32
    ).astype(jnp.bfloat16)
    returned = lax.all_to_all(
        drows.reshape(num_experts, SLOTS, width), "expert", split_axis=0, concat_axis=0, tiled=True
    ).reshape(rows, width)
    token_grads = lax.dot_general(
        one_hot_rows(routed * SLOTS + slots, rows), returned, (((0,), (0,)), ((), ())), preferred_element_type=jnp.float32
    ).astype(jnp.bfloat16)

    halves = [merge(f, to_keep, gots[f], dgu, hidden, rows_x, rows_dy) for f in range(4)]
    for step in range(1, 4):
        for f, (first_axis, first_odd) in enumerate(FLOWS):
            axis = first_axis if step < 2 else 1 - first_axis
            odd = first_odd if step % 2 == 0 else not first_odd
            give, keep = halves[f]
            got = lax.ppermute(give, "dp", pair_perm(axis, odd))
            if step == 3:
                halves[f] = (got, keep)
                continue
            n = keep.shape[1] // 2
            halves[f] = tuple(
                (k.astype(jnp.float32) + g.astype(jnp.float32)).astype(jnp.bfloat16)
                for k, g in ((keep[:, :n], got[:, :n]), (keep[:, n:], got[:, n:]))
            )
    grad_gate_up, grad_down_t = finish([h[1] for h in halves], [h[0] for h in halves])
    return (token_grads, grad_gate_up[None], grad_down_t[None])


def solution(mesh):
    return jax.shard_map(
        local,
        mesh=mesh,
        in_specs=(
            P(("dp", "expert"), None),
            P(("dp", "expert"), None),
            P(("dp", "expert"), None),
            P("expert", None, None),
            P("expert", None, None),
        ),
        out_specs=(P(("dp", "expert"), None), P("expert", "dp", None), P("expert", "dp", None)),
        check_vma=False,
    )
```

```python
import jax
import jax.numpy as jnp
from jax import lax
from jax.experimental import pallas as pl
from jax.experimental.pallas import tpu as pltpu
from jax.sharding import PartitionSpec as P

SLOTS = 32
SIDE = 4
LANE = 128
CHUNKS = 4
FLOWS = ((0, False), (0, True), (1, False), (1, True))
LARGE = pl.CostEstimate(flops=20000000000, bytes_accessed=10000000, transcendentals=0)
SMALL = pl.CostEstimate(flops=1000000, bytes_accessed=100000, transcendentals=0)


def token_slots(routed):
    rows = routed.shape[0]
    places = jnp.arange(rows, dtype=jnp.int32)
    same = (routed[:, None] == routed[None, :]) & (places[:, None] < places[None, :])
    return jnp.sum(same.astype(jnp.int32), axis=0)


def one_hot_rows(target, count):
    spots = jnp.arange(count, dtype=jnp.int32)
    return (spots[:, None] == target[None, :]).astype(jnp.bfloat16)


def feature_blocks(ref, table, f, chunk):
    pair = [
        ref[:, pl.ds(pl.multiple_of(table[f, 2 * chunk + k] * LANE, LANE), LANE)] for k in range(2)
    ]
    return jnp.concatenate(pair, axis=1)


def lanes(chunk):
    return pl.ds(pl.multiple_of(chunk * (2 * LANE), 2 * LANE), 2 * LANE)


def dot32(left, right):
    return jnp.dot(left, right, preferred_element_type=jnp.float32)


def product(left, right):
    return dot32(left, right).astype(jnp.bfloat16)


def flow_parts(f, per, split):
    low, high = f * per, (f + 1) * per
    parts = []
    if low < split:
        parts.append((True, low, min(high, split) - low, 0))
    if high > split:
        begin = max(low, split)
        parts.append((False, begin - split, high - begin, begin - low))
    return parts


def join_kernel(order, places, *refs):
    pieces, outs, sems = refs[: len(order)], refs[len(order) : -1], refs[-1]
    copies = []
    for d, piece in zip(order, pieces):
        for k in range(2):
            row = pl.multiple_of(places[2 * d + k] * SLOTS, SLOTS)
            for n, out in enumerate(outs):
                copies.append(
                    pltpu.make_async_copy(piece.at[n, k], out.at[pl.ds(row, SLOTS)], sems.at[n, 2 * d + k])
                )
    for copy in copies:
        copy.start()
    for copy in copies:
        copy.wait()


def join(order, places, pieces):
    width = pieces[0].shape[3]
    rows = 2 * len(pieces) * SLOTS
    return pl.pallas_call(
        lambda *refs: join_kernel(order, *refs),
        in_specs=[pl.BlockSpec(memory_space=pltpu.SMEM)] + [pl.BlockSpec(memory_space=pl.ANY)] * len(pieces),
        out_specs=[pl.BlockSpec(memory_space=pltpu.VMEM)] * 2,
        out_shape=[jax.ShapeDtypeStruct((rows, width), jnp.bfloat16)] * 2,
        scratch_shapes=[pltpu.SemaphoreType.DMA((2, 2 * len(pieces)))],
        compiler_params=pltpu.CompilerParams(vmem_limit_bytes=8 * 1024 * 1024),
        cost_estimate=SMALL,
        name="join",
    )(places, *pieces)


def gives_kernel(table, gate_up_ref, dhidden_ref, x_ref, dy_ref, dgu_ref, hid_ref, *refs):
    n = len(FLOWS)
    outs, stages, sems = refs[:n], refs[n : 2 * n], refs[2 * n]
    per = outs[0].shape[0]
    ff = dhidden_ref.shape[0]
    tile = 64

    def gradients(i, carry):
        part = pl.ds(pl.multiple_of(i * tile, tile), tile)
        lower = pl.ds(pl.multiple_of(ff + i * tile, tile), tile)
        gate, upper, dhidden = gate_up_ref[part, :], gate_up_ref[lower, :], dhidden_ref[part, :]
        sig = jax.nn.sigmoid(gate)
        silu = gate * sig
        hid_ref[part, :] = (silu * upper).astype(jnp.bfloat16)
        dgu_ref[part, :] = (dhidden * upper * sig * (1.0 + gate * (1.0 - sig))).astype(jnp.bfloat16)
        dgu_ref[lower, :] = (dhidden * silu).astype(jnp.bfloat16)
        return carry

    lax.fori_loop(0, ff // tile, gradients, 0)

    def copy(f, chunk):
        return pltpu.make_async_copy(
            stages[f].at[:, lanes(chunk)], outs[f].at[:, lanes(chunk)], sems.at[f, chunk]
        )

    for f in range(n):

        def body(chunk, carry):
            for from_dgu, first, count, row in flow_parts(f, per, 2 * ff):
                left, right = (dgu_ref, x_ref) if from_dgu else (hid_ref, dy_ref)
                stages[f][row : row + count, lanes(chunk)] = product(
                    left[first : first + count, :], feature_blocks(right, table, f, chunk)
                )
            copy(f, chunk).start()
            return carry

        lax.fori_loop(0, CHUNKS, body, 0)
    for f in range(n):
        for chunk in range(CHUNKS):
            copy(f, chunk).wait()


def make_gives(table, gate_up, dhidden, rows_x, rows_dy):
    ff, rows = dhidden.shape
    size = (3 * ff // 4, 2 * CHUNKS * LANE)
    whole = pl.BlockSpec(memory_space=pltpu.VMEM)
    n = len(FLOWS)
    return pl.pallas_call(
        gives_kernel,
        in_specs=[pl.BlockSpec(memory_space=pltpu.SMEM)] + [whole] * 4,
        out_specs=[whole] * 2 + [pl.BlockSpec(memory_space=pl.ANY)] * n,
        out_shape=[
            jax.ShapeDtypeStruct((2 * ff, rows), jnp.bfloat16),
            jax.ShapeDtypeStruct((ff, rows), jnp.bfloat16),
        ]
        + [jax.ShapeDtypeStruct(size, jnp.bfloat16)] * n,
        scratch_shapes=[pltpu.VMEM(size, jnp.bfloat16)] * n + [pltpu.SemaphoreType.DMA((n, CHUNKS))],
        compiler_params=pltpu.CompilerParams(vmem_limit_bytes=16 * 1024 * 1024),
        cost_estimate=SMALL,
        name="give",
    )(table, gate_up, dhidden, rows_x, rows_dy)


def merge_kernel(f, table, got_ref, *refs):
    *sides, give_ref, keep_ref = refs
    per = give_ref.shape[0]
    half = CHUNKS // 2
    for out, base in ((give_ref, 0), (keep_ref, half)):

        def body(i, carry):
            chunk = base + i
            for k, (_, first, count, row) in enumerate(flow_parts(f, per, 8 * per // 3)):
                total = dot32(
                    sides[2 * k][first : first + count, :], feature_blocks(sides[2 * k + 1], table, f, chunk)
                )
                total += got_ref[row : row + count, lanes(chunk)].astype(jnp.float32)
                out[row : row + count, lanes(i)] = total.astype(jnp.bfloat16)
            return carry

        lax.fori_loop(0, half, body, 0)


def merge(f, table, got, dgu, hidden, rows_x, rows_dy):
    per = got.shape[0]
    sides = []
    for from_dgu, *_ in flow_parts(f, per, dgu.shape[0]):
        sides += [dgu, rows_x] if from_dgu else [hidden, rows_dy]
    whole = pl.BlockSpec(memory_space=pltpu.VMEM)
    return pl.pallas_call(
        lambda *refs: merge_kernel(f, *refs),
        in_specs=[pl.BlockSpec(memory_space=pltpu.SMEM)] + [whole] * (1 + len(sides)),
        out_specs=[whole] * 2,
        out_shape=[jax.ShapeDtypeStruct((per, CHUNKS * LANE), jnp.bfloat16)] * 2,
        compiler_params=pltpu.CompilerParams(vmem_limit_bytes=12 * 1024 * 1024),
        cost_estimate=LARGE,
        name="merge",
    )(table, got, *sides)


def finish_kernel(*refs):
    *parts, up_ref, down_ref = refs
    n = len(parts) // 2
    total = jnp.concatenate(
        [parts[i][...].astype(jnp.float32) + parts[n + i][...].astype(jnp.float32) for i in range(n)], axis=0
    )
    split = up_ref.shape[1]
    up_ref[...] = total[:split].T.astype(jnp.bfloat16)
    down_ref[...] = total[split:].T.astype(jnp.bfloat16)


def finish(keeps, gots):
    per, lane = keeps[0].shape
    whole = pl.BlockSpec(memory_space=pltpu.VMEM)
    return pl.pallas_call(
        finish_kernel,
        in_specs=[whole] * 8,
        out_specs=[whole] * 2,
        out_shape=[
            jax.ShapeDtypeStruct((lane, 8 * per // 3), jnp.bfloat16),
            jax.ShapeDtypeStruct((lane, 4 * per // 3), jnp.bfloat16),
        ],
        compiler_params=pltpu.CompilerParams(vmem_limit_bytes=12 * 1024 * 1024),
        cost_estimate=SMALL,
        name="finish",
    )(*keeps, *gots)


def mate(i, odd):
    return (3 - i) if odd else (i ^ 1)


def pair_perm(axis, odd):
    return [
        (x * SIDE + y, mate(x, odd) * SIDE + y if axis == 0 else x * SIDE + mate(y, odd))
        for x in range(SIDE)
        for y in range(SIDE)
    ]


def first_table(at, axis, odd):
    a, b = at[axis], at[1 - axis]

    def kept(i):
        return [mate(i, not odd), i]

    minor = jnp.stack(kept(mate(b, odd)) + kept(b)).astype(jnp.int32)

    def blocks(i):
        major = jnp.stack(kept(i)).astype(jnp.int32)
        ids = major[:, None] * SIDE + minor[None, :] if axis == 0 else minor[None, :] * SIDE + major[:, None]
        return ids.reshape(-1)

    return blocks(mate(a, odd)), blocks(a)


def local(tokens, out_grads, expert_ids, w_gate_up, w_down_t):
    num_experts = lax.axis_size("expert")
    chips = num_experts // 2
    width = tokens.shape[1]
    ff = w_down_t.shape[2]
    rows = num_experts * SLOTS
    place = lax.axis_index("expert")
    chip, core = place // 2, place % 2
    routed = expert_ids[:, 0]
    slots = token_slots(routed)
    relative = ((routed // 2 - chip + chips) % chips) * SLOTS + slots
    own = routed % 2 == core
    mine_rows = one_hot_rows(jnp.where(own, relative, -1), chips * SLOTS)
    other_rows = one_hot_rows(jnp.where(own, -1, relative), chips * SLOTS)
    distance = jnp.arange(chips, dtype=jnp.int32)
    places = (
        ((chip - distance + chips) % chips)[:, None] * 2
        + jnp.array([0, 1], jnp.int32)[None, :] * (1 - 2 * core)
        + core
    ).reshape(-1)

    def pack(table, values):
        packed = jnp.dot(table, values, preferred_element_type=jnp.float32)
        return packed.astype(jnp.bfloat16).reshape(chips, SLOTS, width)

    swap = [(i, i ^ 1) for i in range(num_experts)]
    sides = [
        (pack(mine_rows, values), lax.ppermute(pack(other_rows, values), "expert", swap))
        for values in (tokens, out_grads)
    ]

    def piece(d):
        return jnp.concatenate([side[d] for pair in sides for side in pair]).reshape(2, 2, SLOTS, width)

    order = (0, 3, 5, 2, 6, 1, 7, 4)
    pieces = [piece(0)]
    for d in order[1:]:
        pieces.append(
            lax.ppermute(
                piece(d), "expert", [(i, (i + 2 * d) % num_experts) for i in range(num_experts)]
            )
        )
    rows_x, rows_dy = join(order, places, pieces)
    w_in = w_gate_up[0]
    w_out = w_down_t[0]

    gate_up = lax.dot_general(
        w_in, rows_x, (((0,), (1,)), ((), ())), preferred_element_type=jnp.float32
    )
    dhidden = lax.dot_general(
        w_out, rows_dy, (((0,), (1,)), ((), ())), preferred_element_type=jnp.float32
    )
    me = lax.axis_index("dp")
    at = (me // SIDE, me % SIDE)
    tables = [first_table(at, axis, odd) for axis, odd in FLOWS]

    to_give = jnp.stack([t[0] for t in tables])
    to_keep = jnp.stack([t[1] for t in tables])
    dgu, hidden, *gives = make_gives(to_give, gate_up, dhidden, rows_x, rows_dy)
    gots = [None] * 4
    for f in (3, 0, 1, 2):
        gots[f] = lax.ppermute(gives[f], "dp", pair_perm(*FLOWS[f]))
    drows = lax.dot_general(
        dgu, w_in, (((0,), (1,)), ((), ())), preferred_element_type=jnp.float32
    ).astype(jnp.bfloat16)
    returned = lax.all_to_all(
        drows.reshape(num_experts, SLOTS, width), "expert", split_axis=0, concat_axis=0, tiled=True
    ).reshape(rows, width)
    token_grads = lax.dot_general(
        one_hot_rows(routed * SLOTS + slots, rows), returned, (((0,), (0,)), ((), ())), preferred_element_type=jnp.float32
    ).astype(jnp.bfloat16)

    halves = [merge(f, to_keep, gots[f], dgu, hidden, rows_x, rows_dy) for f in range(4)]
    for step in range(1, 4):
        for f, (first_axis, first_odd) in enumerate(FLOWS):
            axis = first_axis if step < 2 else 1 - first_axis
            odd = first_odd if step % 2 == 0 else not first_odd
            give, keep = halves[f]
            got = lax.ppermute(give, "dp", pair_perm(axis, odd))
            if step == 3:
                halves[f] = (got, keep)
                continue
            n = keep.shape[1] // 2
            halves[f] = tuple(
                (k.astype(jnp.float32) + g.astype(jnp.float32)).astype(jnp.bfloat16)
                for k, g in ((keep[:, :n], got[:, :n]), (keep[:, n:], got[:, n:]))
            )
    grad_gate_up, grad_down_t = finish([h[1] for h in halves], [h[0] for h in halves])
    return (token_grads, grad_gate_up[None], grad_down_t[None])


def solution(mesh):
    return jax.shard_map(
        local,
        mesh=mesh,
        in_specs=(
            P(("dp", "expert"), None),
            P(("dp", "expert"), None),
            P(("dp", "expert"), None),
            P("expert", None, None),
            P("expert", None, None),
        ),
        out_specs=(P(("dp", "expert"), None), P("expert", "dp", None), P("expert", "dp", None)),
        check_vma=False,
    )
```

```python
import jax
import jax.numpy as jnp
from jax import lax
from jax.experimental import pallas as pl
from jax.experimental.pallas import tpu as pltpu
from jax.sharding import PartitionSpec as P

SLOTS = 32
SIDE = 4
LANE = 128
GIVE_MIB = 40
CHUNKS = 4
FLOWS = ((0, False), (0, True), (1, False), (1, True))
FINISH = pl.CostEstimate(flops=5000000000, bytes_accessed=100000, transcendentals=0)
SMALL = pl.CostEstimate(flops=1000000, bytes_accessed=100000, transcendentals=0)


def pack_kernel(ids_ref, values_ref, out_ref, target_ref):
    ids = ids_ref[...]
    tokens = ids.shape[1]
    experts = out_ref.shape[0] // SLOTS
    mine = (lax.broadcasted_iota(jnp.int32, (experts, tokens), 0) == ids).astype(jnp.float32)
    earlier = lax.broadcasted_iota(jnp.int32, (tokens, tokens), 0) < lax.broadcasted_iota(
        jnp.int32, (tokens, tokens), 1
    )
    before = dot32(mine.astype(jnp.bfloat16), earlier.astype(jnp.bfloat16))
    slots = jnp.sum(before * mine, axis=0, keepdims=True).astype(jnp.int32)
    target = ids * SLOTS + slots
    target_ref[...] = target
    spots = lax.broadcasted_iota(jnp.int32, (out_ref.shape[0], tokens), 0)
    out_ref[...] = product((spots == target).astype(jnp.bfloat16), values_ref[...])


def pack(ids, values, experts):
    tokens, width = values.shape
    tile = 512
    return pl.pallas_call(
        pack_kernel,
        grid=(width // tile,),
        in_specs=[
            pl.BlockSpec((1, tokens), lambda i: (0, 0)),
            pl.BlockSpec((tokens, tile), lambda i: (0, i)),
        ],
        out_specs=[
            pl.BlockSpec((experts * SLOTS, tile), lambda i: (0, i)),
            pl.BlockSpec((1, tokens), lambda i: (0, 0)),
        ],
        out_shape=[
            jax.ShapeDtypeStruct((experts * SLOTS, width), jnp.bfloat16),
            jax.ShapeDtypeStruct((1, tokens), jnp.int32),
        ],
        compiler_params=pltpu.CompilerParams(vmem_limit_bytes=56 * 1024 * 1024),
        cost_estimate=SMALL,
        name="pack",
    )(ids, values)


def feature_blocks(ref, table, f, chunk):
    pair = [
        ref[:, pl.ds(pl.multiple_of(table[f, 2 * chunk + k] * LANE, LANE), LANE)] for k in range(2)
    ]
    return jnp.concatenate(pair, axis=1)


def lanes(chunk):
    return pl.ds(pl.multiple_of(chunk * (2 * LANE), 2 * LANE), 2 * LANE)


def dot32(left, right):
    return jnp.dot(left, right, preferred_element_type=jnp.float32)


def product(left, right):
    return dot32(left, right).astype(jnp.bfloat16)


def flow_parts(f, per, split):
    low, high = f * per, (f + 1) * per
    parts = []
    if low < split:
        parts.append((True, low, min(high, split) - low, 0))
    if high > split:
        begin = max(low, split)
        parts.append((False, begin - split, high - begin, begin - low))
    return parts


def gives_kernel(table, w_ref, hid_ref, x_ref, slope_in, silu_in, dy_in, dgu_ref, dy_ref, *refs):
    n = len(FLOWS)
    outs, stages, (slope_ref, silu_ref, sems, in_sems) = refs[:n], refs[n : 2 * n], refs[2 * n :]
    per = outs[0].shape[0]
    ff = hid_ref.shape[0]
    tile = 256
    part = dy_in.shape[0] // 4
    arrivals = [
        pltpu.make_async_copy(dy_in.at[pl.ds(k * part, part)], dy_ref.at[pl.ds(k * part, part)], in_sems.at[k])
        for k in range(4)
    ]
    factors = [
        pltpu.make_async_copy(slope_in, slope_ref, in_sems.at[4]),
        pltpu.make_async_copy(silu_in, silu_ref, in_sems.at[5]),
    ]
    for copy in arrivals + factors:
        copy.start()
    for copy in arrivals:
        copy.wait()

    def copy(f, chunk):
        return pltpu.make_async_copy(
            stages[f].at[:, lanes(chunk)], outs[f].at[:, lanes(chunk)], sems.at[f, chunk]
        )

    def give(f):
        def body(chunk, carry):
            for from_dgu, first, count, row in flow_parts(f, per, 2 * ff):
                left, right = (dgu_ref, x_ref) if from_dgu else (hid_ref, dy_ref)
                stages[f][row : row + count, lanes(chunk)] = product(
                    left[first : first + count, :], feature_blocks(right, table, f, chunk)
                )
            copy(f, chunk).start()
            return carry

        lax.fori_loop(0, CHUNKS, body, 0, unroll=True)

    give(3)
    for copy_in in factors:
        copy_in.wait()
    for low in range(0, ff, tile):
        here = slice(low, low + tile)
        dhidden = lax.dot_general(
            w_ref[here, :], dy_ref[...], (((1,), (1,)), ((), ())), preferred_element_type=jnp.float32
        )
        dgu_ref[here, :] = (dhidden * slope_ref[here, :]).astype(jnp.bfloat16)
        dgu_ref[ff + low : ff + low + tile, :] = (dhidden * silu_ref[here, :]).astype(jnp.bfloat16)
    for f in range(3):
        give(f)
    for f in range(n):
        for chunk in range(CHUNKS):
            copy(f, chunk).wait()


def make_gives(table, w_out_t, slope, silu, hidden, rows_x, rows_dy):
    ff, rows = hidden.shape
    size = (3 * ff // 4, 2 * CHUNKS * LANE)
    whole = pl.BlockSpec(memory_space=pltpu.VMEM)
    away = pl.BlockSpec(memory_space=pl.ANY)
    n = len(FLOWS)
    return pl.pallas_call(
        gives_kernel,
        in_specs=[pl.BlockSpec(memory_space=pltpu.SMEM)] + [whole] * 3 + [away] * 3,
        out_specs=[whole] * 2 + [away] * n,
        out_shape=[
            jax.ShapeDtypeStruct((2 * ff, rows), jnp.bfloat16),
            jax.ShapeDtypeStruct(rows_dy.shape, jnp.bfloat16),
        ]
        + [jax.ShapeDtypeStruct(size, jnp.bfloat16)] * n,
        scratch_shapes=[pltpu.VMEM(size, jnp.bfloat16)] * n
        + [pltpu.VMEM((ff, rows), jnp.float32)] * 2
        + [pltpu.SemaphoreType.DMA((n, CHUNKS)), pltpu.SemaphoreType.DMA((6,))],
        compiler_params=pltpu.CompilerParams(vmem_limit_bytes=GIVE_MIB * 1024 * 1024),
        cost_estimate=SMALL,
        name="give",
    )(table, w_out_t, hidden, rows_x, slope, silu, rows_dy)


def keeps_kernel(table, dgu_ref, hid_ref, x_ref, dy_ref, *outs):
    per = outs[0].shape[0]
    for f, out in enumerate(outs):

        def body(chunk, carry):
            for from_dgu, first, count, row in flow_parts(f, per, dgu_ref.shape[0]):
                left, right = (dgu_ref, x_ref) if from_dgu else (hid_ref, dy_ref)
                out[row : row + count, lanes(chunk)] = product(
                    left[first : first + count, :], feature_blocks(right, table, f, chunk)
                )
            return carry

        lax.fori_loop(0, CHUNKS, body, 0, unroll=True)


def make_keeps(table, dgu, hidden, rows_x, rows_dy):
    size = (3 * hidden.shape[0] // 4, 2 * CHUNKS * LANE)
    whole = pl.BlockSpec(memory_space=pltpu.VMEM)
    n = len(FLOWS)
    return pl.pallas_call(
        keeps_kernel,
        in_specs=[pl.BlockSpec(memory_space=pltpu.SMEM)] + [whole] * 4,
        out_specs=[whole] * n,
        out_shape=[jax.ShapeDtypeStruct(size, jnp.bfloat16)] * n,
        compiler_params=pltpu.CompilerParams(vmem_limit_bytes=8 * 1024 * 1024),
        cost_estimate=SMALL,
        name="keep",
    )(table, dgu, hidden, rows_x, rows_dy)


def drows_kernel(g_ref, w_ref, out_ref, turned):
    @pl.when(pl.program_id(0) == 0)
    def _():
        turned[...] = g_ref[...].T

    out_ref[...] = lax.dot_general(
        turned[...], w_ref[...], (((1,), (1,)), ((), ())), preferred_element_type=jnp.float32
    ).astype(jnp.bfloat16)


def make_drows(dgu_t, w_in):
    ff2, rows = dgu_t.shape
    width = w_in.shape[0]
    tile = 512
    return pl.pallas_call(
        drows_kernel,
        grid=(width // tile,),
        in_specs=[
            pl.BlockSpec((ff2, rows), lambda i: (0, 0)),
            pl.BlockSpec((tile, ff2), lambda i: (i, 0)),
        ],
        out_specs=pl.BlockSpec((rows, tile), lambda i: (0, i)),
        out_shape=jax.ShapeDtypeStruct((rows, width), jnp.bfloat16),
        scratch_shapes=[pltpu.VMEM((rows, ff2), jnp.bfloat16)],
        compiler_params=pltpu.CompilerParams(vmem_limit_bytes=16 * 1024 * 1024),
        cost_estimate=SMALL,
        name="drows",
    )(dgu_t, w_in)


def finish_kernel(*refs):
    *parts, up_ref, down_ref = refs
    n = len(parts) // 2
    total = jnp.concatenate(
        [parts[i][...].astype(jnp.float32) + parts[n + i][...].astype(jnp.float32) for i in range(n)], axis=0
    )
    split = up_ref.shape[1]
    up_ref[...] = total[:split].T.astype(jnp.bfloat16)
    down_ref[...] = total[split:].T.astype(jnp.bfloat16)


def finish(keeps, gots):
    per, lane = keeps[0].shape
    whole = pl.BlockSpec(memory_space=pltpu.VMEM)
    return pl.pallas_call(
        finish_kernel,
        in_specs=[whole] * 8,
        out_specs=[whole] * 2,
        out_shape=[
            jax.ShapeDtypeStruct((lane, 8 * per // 3), jnp.bfloat16),
            jax.ShapeDtypeStruct((lane, 4 * per // 3), jnp.bfloat16),
        ],
        compiler_params=pltpu.CompilerParams(vmem_limit_bytes=12 * 1024 * 1024),
        cost_estimate=FINISH,
        name="finish",
    )(*keeps, *gots)


def mate(i, odd):
    return (3 - i) if odd else (i ^ 1)


def pair_perm(axis, odd):
    return [
        (x * SIDE + y, mate(x, odd) * SIDE + y if axis == 0 else x * SIDE + mate(y, odd))
        for x in range(SIDE)
        for y in range(SIDE)
    ]


def first_table(at, axis, odd):
    a, b = at[axis], at[1 - axis]

    def kept(i):
        return [mate(i, not odd), i]

    minor = jnp.stack(kept(mate(b, odd)) + kept(b)).astype(jnp.int32)

    def blocks(i):
        major = jnp.stack(kept(i)).astype(jnp.int32)
        ids = major[:, None] * SIDE + minor[None, :] if axis == 0 else minor[None, :] * SIDE + major[:, None]
        return ids.reshape(-1)

    return blocks(mate(a, odd)), blocks(a)


def local(tokens, out_grads, expert_ids, w_gate_up, w_down_t):
    num_experts = lax.axis_size("expert")
    width = tokens.shape[1]
    ff = w_down_t.shape[2]
    rows = num_experts * SLOTS
    ids = expert_ids.reshape(1, -1)

    def send(packed):
        packed = packed.reshape(num_experts, SLOTS, width)
        got = lax.all_to_all(packed, "expert", split_axis=0, concat_axis=0, tiled=True)
        return got.reshape(rows, width)

    packed_x, target = pack(ids, tokens, num_experts)
    packed_dy, _ = pack(ids, out_grads, num_experts)
    rows_x = send(packed_x)
    rows_x, packed_dy = lax.optimization_barrier((rows_x, packed_dy))
    rows_dy = send(packed_dy)
    w_in = w_gate_up[0]
    w_out_t = w_down_t[0].T

    gate_up = lax.dot_general(
        w_in, rows_x, (((0,), (1,)), ((), ())), preferred_element_type=jnp.float32
    )
    gate = gate_up[:ff]
    upper = gate_up[ff:]
    sig = jax.nn.sigmoid(gate)
    silu = gate * sig
    hidden = (silu * upper).astype(jnp.bfloat16)
    slope = upper * sig * (1.0 + gate * (1.0 - sig))

    me = lax.axis_index("dp")
    at = (me // SIDE, me % SIDE)
    tables = [first_table(at, axis, odd) for axis, odd in FLOWS]

    to_give = jnp.stack([t[0] for t in tables])
    to_keep = jnp.stack([t[1] for t in tables])
    dgu, rows_dy, *gives = make_gives(to_give, w_out_t, slope, silu, hidden, rows_x, rows_dy)
    gots = [None] * 4
    for f in (3, 0, 1, 2):
        gots[f] = lax.ppermute(gives[f], "dp", pair_perm(*FLOWS[f]))
    drows = make_drows(dgu, w_in)
    returned = lax.all_to_all(
        drows.reshape(num_experts, SLOTS, width), "expert", split_axis=0, concat_axis=0, tiled=True
    ).reshape(rows, width)
    spots = jnp.arange(rows, dtype=jnp.int32)
    token_grads = lax.dot_general(
        (spots[:, None] == target).astype(jnp.bfloat16), returned, (((0,), (0,)), ((), ())),
        preferred_element_type=jnp.float32,
    ).astype(jnp.bfloat16)

    def add_halves(keep, got):
        n = keep.shape[1] // 2
        return tuple(
            (k.astype(jnp.float32) + g.astype(jnp.float32)).astype(jnp.bfloat16)
            for k, g in ((keep[:, :n], got[:, :n]), (keep[:, n:], got[:, n:]))
        )

    keeps = make_keeps(to_keep, dgu, hidden, rows_x, rows_dy)
    halves = [add_halves(keep, got) for keep, got in zip(keeps, gots)]
    for step in range(1, 4):
        for f, (first_axis, first_odd) in enumerate(FLOWS):
            axis = first_axis if step < 2 else 1 - first_axis
            odd = first_odd if step % 2 == 0 else not first_odd
            give, keep = halves[f]
            got = lax.ppermute(give, "dp", pair_perm(axis, odd))
            halves[f] = (got, keep) if step == 3 else add_halves(keep, got)
    grad_gate_up, grad_down_t = finish([h[1] for h in halves], [h[0] for h in halves])
    return (token_grads, grad_gate_up[None], grad_down_t[None])


def solution(mesh):
    return jax.shard_map(
        local,
        mesh=mesh,
        in_specs=(
            P(("dp", "expert"), None),
            P(("dp", "expert"), None),
            P(("dp", "expert"), None),
            P("expert", None, None),
            P("expert", None, None),
        ),
        out_specs=(P(("dp", "expert"), None), P("expert", "dp", None), P("expert", "dp", None)),
        check_vma=False,
    )
```

```python
import jax
import jax.numpy as jnp
from jax import lax
from jax.experimental import pallas as pl
from jax.experimental.pallas import tpu as pltpu
from jax.sharding import PartitionSpec as P

SLOTS = 32
SIDE = 4
LANE = 128
GIVE_MIB = 40
CHUNKS = 4
FLOWS = ((0, False), (0, True), (1, False), (1, True))
FINISH = pl.CostEstimate(flops=5000000000, bytes_accessed=100000, transcendentals=0)
SMALL = pl.CostEstimate(flops=1000000, bytes_accessed=100000, transcendentals=0)


def pack_kernel(ids_ref, values_ref, out_ref, target_ref, chosen):
    @pl.when(pl.program_id(0) == 0)
    def _():
        ids = ids_ref[...]
        tokens = ids.shape[1]
        experts = out_ref.shape[0] // SLOTS
        mine = (lax.broadcasted_iota(jnp.int32, (experts, tokens), 0) == ids).astype(jnp.float32)
        earlier = lax.broadcasted_iota(jnp.int32, (tokens, tokens), 0) < lax.broadcasted_iota(
            jnp.int32, (tokens, tokens), 1
        )
        before = dot32(mine.astype(jnp.bfloat16), earlier.astype(jnp.bfloat16))
        slots = jnp.sum(before * mine, axis=0, keepdims=True).astype(jnp.int32)
        target = ids * SLOTS + slots
        target_ref[...] = target
        spots = lax.broadcasted_iota(jnp.int32, (out_ref.shape[0], tokens), 0)
        chosen[...] = (spots == target).astype(jnp.bfloat16)

    out_ref[...] = product(chosen[...], values_ref[...])


def pack(ids, values, experts):
    tokens, width = values.shape
    tile = 512
    return pl.pallas_call(
        pack_kernel,
        grid=(width // tile,),
        in_specs=[
            pl.BlockSpec((1, tokens), lambda i: (0, 0)),
            pl.BlockSpec((tokens, tile), lambda i: (0, i)),
        ],
        out_specs=[
            pl.BlockSpec((experts * SLOTS, tile), lambda i: (0, i)),
            pl.BlockSpec((1, tokens), lambda i: (0, 0)),
        ],
        out_shape=[
            jax.ShapeDtypeStruct((experts * SLOTS, width), jnp.bfloat16),
            jax.ShapeDtypeStruct((1, tokens), jnp.int32),
        ],
        scratch_shapes=[pltpu.VMEM((experts * SLOTS, tokens), jnp.bfloat16)],
        compiler_params=pltpu.CompilerParams(vmem_limit_bytes=56 * 1024 * 1024),
        cost_estimate=SMALL,
        name="pack",
    )(ids, values)


def feature_blocks(ref, table, f, chunk):
    pair = [
        ref[:, pl.ds(pl.multiple_of(table[f, 2 * chunk + k] * LANE, LANE), LANE)] for k in range(2)
    ]
    return jnp.concatenate(pair, axis=1)


def lanes(chunk):
    return pl.ds(pl.multiple_of(chunk * (2 * LANE), 2 * LANE), 2 * LANE)


def dot32(left, right):
    return jnp.dot(left, right, preferred_element_type=jnp.float32)


def product(left, right):
    return dot32(left, right).astype(jnp.bfloat16)


def flow_parts(f, per, split):
    low, high = f * per, (f + 1) * per
    parts = []
    if low < split:
        parts.append((True, low, min(high, split) - low, 0))
    if high > split:
        begin = max(low, split)
        parts.append((False, begin - split, high - begin, begin - low))
    return parts


def gives_kernel(table, w_ref, hid_ref, x_ref, slope_in, silu_in, dy_in, dgu_ref, dy_ref, *refs):
    n = len(FLOWS)
    outs, stages, (slope_ref, silu_ref, sems, in_sems) = refs[:n], refs[n : 2 * n], refs[2 * n :]
    per = outs[0].shape[0]
    ff = hid_ref.shape[0]
    tile = 256
    part = dy_in.shape[0] // 4
    arrivals = [
        pltpu.make_async_copy(dy_in.at[pl.ds(k * part, part)], dy_ref.at[pl.ds(k * part, part)], in_sems.at[k])
        for k in range(4)
    ]
    factors = [
        pltpu.make_async_copy(slope_in, slope_ref, in_sems.at[4]),
        pltpu.make_async_copy(silu_in, silu_ref, in_sems.at[5]),
    ]
    for copy in arrivals + factors:
        copy.start()
    for copy in arrivals:
        copy.wait()

    def copy(f, chunk):
        return pltpu.make_async_copy(
            stages[f].at[:, lanes(chunk)], outs[f].at[:, lanes(chunk)], sems.at[f, chunk]
        )

    def give(f):
        def body(chunk, carry):
            for from_dgu, first, count, row in flow_parts(f, per, 2 * ff):
                left, right = (dgu_ref, x_ref) if from_dgu else (hid_ref, dy_ref)
                stages[f][row : row + count, lanes(chunk)] = product(
                    left[first : first + count, :], feature_blocks(right, table, f, chunk)
                )
            copy(f, chunk).start()
            return carry

        lax.fori_loop(0, CHUNKS, body, 0, unroll=True)

    give(3)
    for copy_in in factors:
        copy_in.wait()
    for low in range(0, ff, tile):
        here = slice(low, low + tile)
        dhidden = lax.dot_general(
            w_ref[here, :], dy_ref[...], (((1,), (1,)), ((), ())), preferred_element_type=jnp.float32
        )
        dgu_ref[here, :] = (dhidden * slope_ref[here, :]).astype(jnp.bfloat16)
        dgu_ref[ff + low : ff + low + tile, :] = (dhidden * silu_ref[here, :]).astype(jnp.bfloat16)
    for f in range(3):
        give(f)
    for f in range(n):
        for chunk in range(CHUNKS):
            copy(f, chunk).wait()


def make_gives(table, w_out_t, slope, silu, hidden, rows_x, rows_dy):
    ff, rows = hidden.shape
    size = (3 * ff // 4, 2 * CHUNKS * LANE)
    whole = pl.BlockSpec(memory_space=pltpu.VMEM)
    away = pl.BlockSpec(memory_space=pl.ANY)
    n = len(FLOWS)
    return pl.pallas_call(
        gives_kernel,
        in_specs=[pl.BlockSpec(memory_space=pltpu.SMEM)] + [whole] * 3 + [away] * 3,
        out_specs=[whole] * 2 + [away] * n,
        out_shape=[
            jax.ShapeDtypeStruct((2 * ff, rows), jnp.bfloat16),
            jax.ShapeDtypeStruct(rows_dy.shape, jnp.bfloat16),
        ]
        + [jax.ShapeDtypeStruct(size, jnp.bfloat16)] * n,
        scratch_shapes=[pltpu.VMEM(size, jnp.bfloat16)] * n
        + [pltpu.VMEM((ff, rows), jnp.bfloat16)] * 2
        + [pltpu.SemaphoreType.DMA((n, CHUNKS)), pltpu.SemaphoreType.DMA((6,))],
        compiler_params=pltpu.CompilerParams(vmem_limit_bytes=GIVE_MIB * 1024 * 1024),
        cost_estimate=SMALL,
        name="give",
    )(table, w_out_t, hidden, rows_x, slope, silu, rows_dy)


def keeps_kernel(table, dgu_ref, hid_ref, x_ref, dy_ref, *outs):
    per = outs[0].shape[0]
    for f, out in enumerate(outs):

        def body(chunk, carry):
            for from_dgu, first, count, row in flow_parts(f, per, dgu_ref.shape[0]):
                left, right = (dgu_ref, x_ref) if from_dgu else (hid_ref, dy_ref)
                out[row : row + count, lanes(chunk)] = product(
                    left[first : first + count, :], feature_blocks(right, table, f, chunk)
                )
            return carry

        lax.fori_loop(0, CHUNKS, body, 0, unroll=True)


def make_keeps(table, dgu, hidden, rows_x, rows_dy):
    size = (3 * hidden.shape[0] // 4, 2 * CHUNKS * LANE)
    whole = pl.BlockSpec(memory_space=pltpu.VMEM)
    n = len(FLOWS)
    return pl.pallas_call(
        keeps_kernel,
        in_specs=[pl.BlockSpec(memory_space=pltpu.SMEM)] + [whole] * 4,
        out_specs=[whole] * n,
        out_shape=[jax.ShapeDtypeStruct(size, jnp.bfloat16)] * n,
        compiler_params=pltpu.CompilerParams(vmem_limit_bytes=8 * 1024 * 1024),
        cost_estimate=SMALL,
        name="keep",
    )(table, dgu, hidden, rows_x, rows_dy)


def drows_kernel(g_ref, w_ref, out_ref, turned):
    @pl.when(pl.program_id(0) == 0)
    def _():
        turned[...] = g_ref[...].T

    out_ref[...] = lax.dot_general(
        turned[...], w_ref[...], (((1,), (1,)), ((), ())), preferred_element_type=jnp.float32
    ).astype(jnp.bfloat16)


def make_drows(dgu_t, w_in):
    ff2, rows = dgu_t.shape
    width = w_in.shape[0]
    tile = 512
    return pl.pallas_call(
        drows_kernel,
        grid=(width // tile,),
        in_specs=[
            pl.BlockSpec((ff2, rows), lambda i: (0, 0)),
            pl.BlockSpec((tile, ff2), lambda i: (i, 0)),
        ],
        out_specs=pl.BlockSpec((rows, tile), lambda i: (0, i)),
        out_shape=jax.ShapeDtypeStruct((rows, width), jnp.bfloat16),
        scratch_shapes=[pltpu.VMEM((rows, ff2), jnp.bfloat16)],
        compiler_params=pltpu.CompilerParams(vmem_limit_bytes=16 * 1024 * 1024),
        cost_estimate=SMALL,
        name="drows",
    )(dgu_t, w_in)


def finish_kernel(*refs):
    *parts, up_ref, down_ref = refs
    n = len(parts) // 2
    total = jnp.concatenate(
        [parts[i][...].astype(jnp.float32) + parts[n + i][...].astype(jnp.float32) for i in range(n)], axis=0
    )
    split = up_ref.shape[1]
    up_ref[...] = total[:split].T.astype(jnp.bfloat16)
    down_ref[...] = total[split:].T.astype(jnp.bfloat16)


def finish(keeps, gots):
    per, lane = keeps[0].shape
    whole = pl.BlockSpec(memory_space=pltpu.VMEM)
    return pl.pallas_call(
        finish_kernel,
        in_specs=[whole] * 8,
        out_specs=[whole] * 2,
        out_shape=[
            jax.ShapeDtypeStruct((lane, 8 * per // 3), jnp.bfloat16),
            jax.ShapeDtypeStruct((lane, 4 * per // 3), jnp.bfloat16),
        ],
        compiler_params=pltpu.CompilerParams(vmem_limit_bytes=12 * 1024 * 1024),
        cost_estimate=FINISH,
        name="finish",
    )(*keeps, *gots)


def mate(i, odd):
    return (3 - i) if odd else (i ^ 1)


def pair_perm(axis, odd):
    return [
        (x * SIDE + y, mate(x, odd) * SIDE + y if axis == 0 else x * SIDE + mate(y, odd))
        for x in range(SIDE)
        for y in range(SIDE)
    ]


def first_table(at, axis, odd):
    a, b = at[axis], at[1 - axis]

    def kept(i):
        return [mate(i, not odd), i]

    minor = jnp.stack(kept(mate(b, odd)) + kept(b)).astype(jnp.int32)

    def blocks(i):
        major = jnp.stack(kept(i)).astype(jnp.int32)
        ids = major[:, None] * SIDE + minor[None, :] if axis == 0 else minor[None, :] * SIDE + major[:, None]
        return ids.reshape(-1)

    return blocks(mate(a, odd)), blocks(a)


def local(tokens, out_grads, expert_ids, w_gate_up, w_down_t):
    num_experts = lax.axis_size("expert")
    width = tokens.shape[1]
    ff = w_down_t.shape[2]
    rows = num_experts * SLOTS
    ids = expert_ids.reshape(1, -1)

    def send(packed):
        packed = packed.reshape(num_experts, SLOTS, width)
        got = lax.all_to_all(packed, "expert", split_axis=0, concat_axis=0, tiled=True)
        return got.reshape(rows, width)

    packed_x, target = pack(ids, tokens, num_experts)
    packed_dy, _ = pack(ids, out_grads, num_experts)
    rows_x = send(packed_x)
    rows_x, packed_dy = lax.optimization_barrier((rows_x, packed_dy))
    rows_dy = send(packed_dy)
    w_in = w_gate_up[0]
    w_out_t = w_down_t[0].T

    gate_up = lax.dot_general(
        w_in, rows_x, (((0,), (1,)), ((), ())), preferred_element_type=jnp.float32
    )
    gate = gate_up[:ff]
    upper = gate_up[ff:]
    sig = jax.nn.sigmoid(gate)
    silu = gate * sig
    hidden = (silu * upper).astype(jnp.bfloat16)
    slope = (upper * sig * (1.0 + gate * (1.0 - sig))).astype(jnp.bfloat16)
    silu = silu.astype(jnp.bfloat16)

    me = lax.axis_index("dp")
    at = (me // SIDE, me % SIDE)
    tables = [first_table(at, axis, odd) for axis, odd in FLOWS]

    to_give = jnp.stack([t[0] for t in tables])
    to_keep = jnp.stack([t[1] for t in tables])
    dgu, rows_dy, *gives = make_gives(to_give, w_out_t, slope, silu, hidden, rows_x, rows_dy)
    gots = [None] * 4
    for f in (3, 0, 1, 2):
        gots[f] = lax.ppermute(gives[f], "dp", pair_perm(*FLOWS[f]))
    drows = make_drows(dgu, w_in)
    returned = lax.all_to_all(
        drows.reshape(num_experts, SLOTS, width), "expert", split_axis=0, concat_axis=0, tiled=True
    ).reshape(rows, width)
    spots = jnp.arange(rows, dtype=jnp.int32)
    token_grads = lax.dot_general(
        (spots[:, None] == target).astype(jnp.bfloat16), returned, (((0,), (0,)), ((), ())),
        preferred_element_type=jnp.float32,
    ).astype(jnp.bfloat16)

    def add_halves(keep, got):
        n = keep.shape[1] // 2
        return tuple(
            k + g
            for k, g in ((keep[:, :n], got[:, :n]), (keep[:, n:], got[:, n:]))
        )

    keeps = make_keeps(to_keep, dgu, hidden, rows_x, rows_dy)
    halves = [add_halves(keep, got) for keep, got in zip(keeps, gots)]
    for step in range(1, 4):
        for f, (first_axis, first_odd) in enumerate(FLOWS):
            axis = first_axis if step < 2 else 1 - first_axis
            odd = first_odd if step % 2 == 0 else not first_odd
            give, keep = halves[f]
            got = lax.ppermute(give, "dp", pair_perm(axis, odd))
            halves[f] = (got, keep) if step == 3 else add_halves(keep, got)
    grad_gate_up, grad_down_t = finish([h[1] for h in halves], [h[0] for h in halves])
    return (token_grads, grad_gate_up[None], grad_down_t[None])


def solution(mesh):
    return jax.shard_map(
        local,
        mesh=mesh,
        in_specs=(
            P(("dp", "expert"), None),
            P(("dp", "expert"), None),
            P(("dp", "expert"), None),
            P("expert", None, None),
            P("expert", None, None),
        ),
        out_specs=(P(("dp", "expert"), None), P("expert", "dp", None), P("expert", "dp", None)),
        check_vma=False,
    )
```

```python
import jax
import jax.numpy as jnp
from jax import lax
from jax.experimental import pallas as pl
from jax.experimental.pallas import tpu as pltpu
from jax.sharding import PartitionSpec as P

SLOTS = 32
SIDE = 4
LANE = 128
GIVE_MIB = 40
CHUNKS = 4
FLOWS = ((0, False), (0, True), (1, False), (1, True))
FINISH = pl.CostEstimate(flops=5000000000, bytes_accessed=100000, transcendentals=0)
SMALL = pl.CostEstimate(flops=1000000, bytes_accessed=100000, transcendentals=0)


def pack_kernel(ids_ref, values_ref, out_ref, target_ref, chosen):
    @pl.when(pl.program_id(0) == 0)
    def _():
        ids = ids_ref[...]
        tokens = ids.shape[1]
        experts = out_ref.shape[0] // SLOTS
        mine = (lax.broadcasted_iota(jnp.int32, (experts, tokens), 0) == ids).astype(jnp.float32)
        earlier = lax.broadcasted_iota(jnp.int32, (tokens, tokens), 0) < lax.broadcasted_iota(
            jnp.int32, (tokens, tokens), 1
        )
        before = dot32(mine.astype(jnp.bfloat16), earlier.astype(jnp.bfloat16))
        slots = jnp.sum(before * mine, axis=0, keepdims=True).astype(jnp.int32)
        target = ids * SLOTS + slots
        target_ref[...] = target
        spots = lax.broadcasted_iota(jnp.int32, (out_ref.shape[0], tokens), 0)
        chosen[...] = (spots == target).astype(jnp.bfloat16)

    out_ref[...] = product(chosen[...], values_ref[...])


def pack(ids, values, experts):
    tokens, width = values.shape
    tile = 512
    return pl.pallas_call(
        pack_kernel,
        grid=(width // tile,),
        in_specs=[
            pl.BlockSpec((1, tokens), lambda i: (0, 0)),
            pl.BlockSpec((tokens, tile), lambda i: (0, i)),
        ],
        out_specs=[
            pl.BlockSpec((experts * SLOTS, tile), lambda i: (0, i)),
            pl.BlockSpec((1, tokens), lambda i: (0, 0)),
        ],
        out_shape=[
            jax.ShapeDtypeStruct((experts * SLOTS, width), jnp.bfloat16),
            jax.ShapeDtypeStruct((1, tokens), jnp.int32),
        ],
        scratch_shapes=[pltpu.VMEM((experts * SLOTS, tokens), jnp.bfloat16)],
        compiler_params=pltpu.CompilerParams(vmem_limit_bytes=56 * 1024 * 1024),
        cost_estimate=SMALL,
        name="pack",
    )(ids, values)


def feature_blocks(ref, table, f, chunk):
    pair = [
        ref[:, pl.ds(pl.multiple_of(table[f, 2 * chunk + k] * LANE, LANE), LANE)] for k in range(2)
    ]
    return jnp.concatenate(pair, axis=1)


def lanes(chunk):
    return pl.ds(pl.multiple_of(chunk * (2 * LANE), 2 * LANE), 2 * LANE)


def dot32(left, right):
    return jnp.dot(left, right, preferred_element_type=jnp.float32)


def product(left, right):
    return dot32(left, right).astype(jnp.bfloat16)


def flow_parts(f, per, split):
    low, high = f * per, (f + 1) * per
    parts = []
    if low < split:
        parts.append((True, low, min(high, split) - low, 0))
    if high > split:
        begin = max(low, split)
        parts.append((False, begin - split, high - begin, begin - low))
    return parts


def factors_kernel(gate_up_ref, slope_ref, silu_ref, hid_ref):
    ff = hid_ref.shape[0]
    tile = 64

    def body(i, carry):
        part = pl.ds(pl.multiple_of(i * tile, tile), tile)
        gate = gate_up_ref[part, :]
        upper = gate_up_ref[pl.ds(pl.multiple_of(ff + i * tile, tile), tile), :]
        sig = jax.nn.sigmoid(gate)
        silu = gate * sig
        silu_ref[part, :] = silu.astype(jnp.bfloat16)
        hid_ref[part, :] = (silu * upper).astype(jnp.bfloat16)
        slope_ref[part, :] = (upper * sig * (1.0 + gate * (1.0 - sig))).astype(jnp.bfloat16)
        return carry

    lax.fori_loop(0, ff // tile, body, 0)


def make_factors(gate_up):
    whole = pl.BlockSpec(memory_space=pltpu.VMEM)
    return pl.pallas_call(
        factors_kernel,
        in_specs=[whole],
        out_specs=[whole] * 3,
        out_shape=[jax.ShapeDtypeStruct((gate_up.shape[0] // 2, gate_up.shape[1]), jnp.bfloat16)] * 3,
        compiler_params=pltpu.CompilerParams(vmem_limit_bytes=8 * 1024 * 1024),
        cost_estimate=SMALL,
        name="factors",
    )(gate_up)


def gives_kernel(table, w_ref, hid_ref, x_ref, dy_ref, slope_ref, silu_ref, dgu_ref, *refs):
    n = len(FLOWS)
    outs, stages, sems = refs[:n], refs[n : 2 * n], refs[2 * n]
    per = outs[0].shape[0]
    ff = hid_ref.shape[0]
    tile = 256
    def copy(f, chunk):
        return pltpu.make_async_copy(
            stages[f].at[:, lanes(chunk)], outs[f].at[:, lanes(chunk)], sems.at[f, chunk]
        )

    def give(f):
        def body(chunk, carry):
            for from_dgu, first, count, row in flow_parts(f, per, 2 * ff):
                left, right = (dgu_ref, x_ref) if from_dgu else (hid_ref, dy_ref)
                stages[f][row : row + count, lanes(chunk)] = product(
                    left[first : first + count, :], feature_blocks(right, table, f, chunk)
                )
            copy(f, chunk).start()
            return carry

        lax.fori_loop(0, CHUNKS, body, 0, unroll=True)

    give(3)
    for low in range(0, ff, tile):
        here = slice(low, low + tile)
        dhidden = lax.dot_general(
            w_ref[here, :], dy_ref[...], (((1,), (1,)), ((), ())), preferred_element_type=jnp.float32
        )
        dgu_ref[here, :] = (dhidden * slope_ref[here, :]).astype(jnp.bfloat16)
        dgu_ref[ff + low : ff + low + tile, :] = (dhidden * silu_ref[here, :]).astype(jnp.bfloat16)
    for f in range(3):
        give(f)
    for f in range(n):
        for chunk in range(CHUNKS):
            copy(f, chunk).wait()


def make_gives(table, w_out_t, slope, silu, hidden, rows_x, rows_dy):
    ff, rows = hidden.shape
    size = (3 * ff // 4, 2 * CHUNKS * LANE)
    whole = pl.BlockSpec(memory_space=pltpu.VMEM)
    away = pl.BlockSpec(memory_space=pl.ANY)
    n = len(FLOWS)
    return pl.pallas_call(
        gives_kernel,
        in_specs=[pl.BlockSpec(memory_space=pltpu.SMEM)] + [whole] * 6,
        out_specs=[whole] + [away] * n,
        out_shape=[jax.ShapeDtypeStruct((2 * ff, rows), jnp.bfloat16)]
        + [jax.ShapeDtypeStruct(size, jnp.bfloat16)] * n,
        scratch_shapes=[pltpu.VMEM(size, jnp.bfloat16)] * n + [pltpu.SemaphoreType.DMA((n, CHUNKS))],
        compiler_params=pltpu.CompilerParams(vmem_limit_bytes=GIVE_MIB * 1024 * 1024),
        cost_estimate=SMALL,
        name="give",
    )(table, w_out_t, hidden, rows_x, rows_dy, slope, silu)


def keeps_kernel(table, dgu_ref, hid_ref, x_ref, dy_ref, *outs):
    per = outs[0].shape[0]
    for f, out in enumerate(outs):

        def body(chunk, carry):
            for from_dgu, first, count, row in flow_parts(f, per, dgu_ref.shape[0]):
                left, right = (dgu_ref, x_ref) if from_dgu else (hid_ref, dy_ref)
                out[row : row + count, lanes(chunk)] = product(
                    left[first : first + count, :], feature_blocks(right, table, f, chunk)
                )
            return carry

        lax.fori_loop(0, CHUNKS, body, 0, unroll=True)


def make_keeps(table, dgu, hidden, rows_x, rows_dy):
    size = (3 * hidden.shape[0] // 4, 2 * CHUNKS * LANE)
    whole = pl.BlockSpec(memory_space=pltpu.VMEM)
    n = len(FLOWS)
    return pl.pallas_call(
        keeps_kernel,
        in_specs=[pl.BlockSpec(memory_space=pltpu.SMEM)] + [whole] * 4,
        out_specs=[whole] * n,
        out_shape=[jax.ShapeDtypeStruct(size, jnp.bfloat16)] * n,
        compiler_params=pltpu.CompilerParams(vmem_limit_bytes=8 * 1024 * 1024),
        cost_estimate=SMALL,
        name="keep",
    )(table, dgu, hidden, rows_x, rows_dy)


def drows_kernel(g_ref, w_ref, out_ref, turned):
    @pl.when(pl.program_id(0) == 0)
    def _():
        turned[...] = g_ref[...].T

    out_ref[...] = lax.dot_general(
        turned[...], w_ref[...], (((1,), (1,)), ((), ())), preferred_element_type=jnp.float32
    ).astype(jnp.bfloat16)


def make_drows(dgu_t, w_in):
    ff2, rows = dgu_t.shape
    width = w_in.shape[0]
    tile = 512
    return pl.pallas_call(
        drows_kernel,
        grid=(width // tile,),
        in_specs=[
            pl.BlockSpec((ff2, rows), lambda i: (0, 0)),
            pl.BlockSpec((tile, ff2), lambda i: (i, 0)),
        ],
        out_specs=pl.BlockSpec((rows, tile), lambda i: (0, i)),
        out_shape=jax.ShapeDtypeStruct((rows, width), jnp.bfloat16),
        scratch_shapes=[pltpu.VMEM((rows, ff2), jnp.bfloat16)],
        compiler_params=pltpu.CompilerParams(vmem_limit_bytes=16 * 1024 * 1024),
        cost_estimate=SMALL,
        name="drows",
    )(dgu_t, w_in)


def finish_kernel(*refs):
    *parts, up_ref, down_ref = refs
    n = len(parts) // 2
    total = jnp.concatenate(
        [parts[i][...].astype(jnp.float32) + parts[n + i][...].astype(jnp.float32) for i in range(n)], axis=0
    )
    split = up_ref.shape[1]
    up_ref[...] = total[:split].T.astype(jnp.bfloat16)
    down_ref[...] = total[split:].T.astype(jnp.bfloat16)


def finish(keeps, gots):
    per, lane = keeps[0].shape
    whole = pl.BlockSpec(memory_space=pltpu.VMEM)
    return pl.pallas_call(
        finish_kernel,
        in_specs=[whole] * 8,
        out_specs=[whole] * 2,
        out_shape=[
            jax.ShapeDtypeStruct((lane, 8 * per // 3), jnp.bfloat16),
            jax.ShapeDtypeStruct((lane, 4 * per // 3), jnp.bfloat16),
        ],
        compiler_params=pltpu.CompilerParams(vmem_limit_bytes=12 * 1024 * 1024),
        cost_estimate=FINISH,
        name="finish",
    )(*keeps, *gots)


def mate(i, odd):
    return (3 - i) if odd else (i ^ 1)


def pair_perm(axis, odd):
    return [
        (x * SIDE + y, mate(x, odd) * SIDE + y if axis == 0 else x * SIDE + mate(y, odd))
        for x in range(SIDE)
        for y in range(SIDE)
    ]


def first_table(at, axis, odd):
    a, b = at[axis], at[1 - axis]

    def kept(i):
        return [mate(i, not odd), i]

    minor = jnp.stack(kept(mate(b, odd)) + kept(b)).astype(jnp.int32)

    def blocks(i):
        major = jnp.stack(kept(i)).astype(jnp.int32)
        ids = major[:, None] * SIDE + minor[None, :] if axis == 0 else minor[None, :] * SIDE + major[:, None]
        return ids.reshape(-1)

    return blocks(mate(a, odd)), blocks(a)


def local(tokens, out_grads, expert_ids, w_gate_up, w_down_t):
    num_experts = lax.axis_size("expert")
    width = tokens.shape[1]
    ff = w_down_t.shape[2]
    rows = num_experts * SLOTS
    ids = expert_ids.reshape(1, -1)

    def send(packed):
        packed = packed.reshape(num_experts, SLOTS, width)
        got = lax.all_to_all(packed, "expert", split_axis=0, concat_axis=0, tiled=True)
        return got.reshape(rows, width)

    packed_x, target = pack(ids, tokens, num_experts)
    packed_dy, _ = pack(ids, out_grads, num_experts)
    rows_x = send(packed_x)
    rows_x, packed_dy = lax.optimization_barrier((rows_x, packed_dy))
    rows_dy = send(packed_dy)
    w_in = w_gate_up[0]
    w_out_t = w_down_t[0].T

    gate_up = lax.dot_general(
        w_in, rows_x, (((0,), (1,)), ((), ())), preferred_element_type=jnp.float32
    )
    slope, silu, hidden = make_factors(gate_up)

    me = lax.axis_index("dp")
    at = (me // SIDE, me % SIDE)
    tables = [first_table(at, axis, odd) for axis, odd in FLOWS]

    to_give = jnp.stack([t[0] for t in tables])
    to_keep = jnp.stack([t[1] for t in tables])
    dgu, *gives = make_gives(to_give, w_out_t, slope, silu, hidden, rows_x, rows_dy)
    gots = [None] * 4
    for f in (3, 0, 1, 2):
        gots[f] = lax.ppermute(gives[f], "dp", pair_perm(*FLOWS[f]))
    drows = make_drows(dgu, w_in)
    returned = lax.all_to_all(
        drows.reshape(num_experts, SLOTS, width), "expert", split_axis=0, concat_axis=0, tiled=True
    ).reshape(rows, width)
    spots = jnp.arange(rows, dtype=jnp.int32)
    token_grads = lax.dot_general(
        (spots[:, None] == target).astype(jnp.bfloat16), returned, (((0,), (0,)), ((), ())),
        preferred_element_type=jnp.float32,
    ).astype(jnp.bfloat16)

    def add_halves(keep, got):
        n = keep.shape[1] // 2
        return tuple(
            k + g
            for k, g in ((keep[:, :n], got[:, :n]), (keep[:, n:], got[:, n:]))
        )

    keeps = make_keeps(to_keep, dgu, hidden, rows_x, rows_dy)
    halves = [add_halves(keep, got) for keep, got in zip(keeps, gots)]
    for step in range(1, 4):
        for f, (first_axis, first_odd) in enumerate(FLOWS):
            axis = first_axis if step < 2 else 1 - first_axis
            odd = first_odd if step % 2 == 0 else not first_odd
            give, keep = halves[f]
            got = lax.ppermute(give, "dp", pair_perm(axis, odd))
            halves[f] = (got, keep) if step == 3 else add_halves(keep, got)
    grad_gate_up, grad_down_t = finish([h[1] for h in halves], [h[0] for h in halves])
    return (token_grads, grad_gate_up[None], grad_down_t[None])


def solution(mesh):
    return jax.shard_map(
        local,
        mesh=mesh,
        in_specs=(
            P(("dp", "expert"), None),
            P(("dp", "expert"), None),
            P(("dp", "expert"), None),
            P("expert", None, None),
            P("expert", None, None),
        ),
        out_specs=(P(("dp", "expert"), None), P("expert", "dp", None), P("expert", "dp", None)),
        check_vma=False,
    )
```

```python
import jax
import jax.numpy as jnp
from jax import lax
from jax.experimental import pallas as pl
from jax.experimental.pallas import tpu as pltpu
from jax.sharding import PartitionSpec as P

SLOTS = 32
SIDE = 4
LANE = 128
GIVE_MIB = 40
CHUNKS = 4
FLOWS = ((0, False), (0, True), (1, False), (1, True))
FINISH = pl.CostEstimate(flops=5000000000, bytes_accessed=100000, transcendentals=0)
SMALL = pl.CostEstimate(flops=1000000, bytes_accessed=100000, transcendentals=0)


def pack_kernel(ids_ref, values_ref, out_ref, target_ref, chosen):
    @pl.when(pl.program_id(0) == 0)
    def _():
        ids = ids_ref[...]
        tokens = ids.shape[1]
        experts = out_ref.shape[0] // SLOTS
        mine = (lax.broadcasted_iota(jnp.int32, (experts, tokens), 0) == ids).astype(jnp.float32)
        earlier = lax.broadcasted_iota(jnp.int32, (tokens, tokens), 0) < lax.broadcasted_iota(
            jnp.int32, (tokens, tokens), 1
        )
        before = dot32(mine.astype(jnp.bfloat16), earlier.astype(jnp.bfloat16))
        slots = jnp.sum(before * mine, axis=0, keepdims=True).astype(jnp.int32)
        target = ids * SLOTS + slots
        target_ref[...] = target
        spots = lax.broadcasted_iota(jnp.int32, (out_ref.shape[0], tokens), 0)
        chosen[...] = (spots == target).astype(jnp.bfloat16)

    out_ref[...] = product(chosen[...], values_ref[...])


def pack(ids, values, experts):
    tokens, width = values.shape
    tile = 512
    return pl.pallas_call(
        pack_kernel,
        grid=(width // tile,),
        in_specs=[
            pl.BlockSpec((1, tokens), lambda i: (0, 0)),
            pl.BlockSpec((tokens, tile), lambda i: (0, i)),
        ],
        out_specs=[
            pl.BlockSpec((experts * SLOTS, tile), lambda i: (0, i)),
            pl.BlockSpec((1, tokens), lambda i: (0, 0)),
        ],
        out_shape=[
            jax.ShapeDtypeStruct((experts * SLOTS, width), jnp.bfloat16),
            jax.ShapeDtypeStruct((1, tokens), jnp.int32),
        ],
        scratch_shapes=[pltpu.VMEM((experts * SLOTS, tokens), jnp.bfloat16)],
        compiler_params=pltpu.CompilerParams(vmem_limit_bytes=56 * 1024 * 1024),
        cost_estimate=SMALL,
        name="pack",
    )(ids, values)


def feature_blocks(ref, table, f, chunk):
    pair = [
        ref[:, pl.ds(pl.multiple_of(table[f, 2 * chunk + k] * LANE, LANE), LANE)] for k in range(2)
    ]
    return jnp.concatenate(pair, axis=1)


def lanes(chunk):
    return pl.ds(pl.multiple_of(chunk * (2 * LANE), 2 * LANE), 2 * LANE)


def dot32(left, right):
    return jnp.dot(left, right, preferred_element_type=jnp.float32)


def product(left, right):
    return dot32(left, right).astype(jnp.bfloat16)


def flow_parts(f, per, split):
    low, high = f * per, (f + 1) * per
    parts = []
    if low < split:
        parts.append((True, low, min(high, split) - low, 0))
    if high > split:
        begin = max(low, split)
        parts.append((False, begin - split, high - begin, begin - low))
    return parts


def factors_kernel(gate_up_ref, slope_ref, silu_ref, hid_ref):
    ff = hid_ref.shape[0]
    tile = 64

    def body(i, carry):
        part = pl.ds(pl.multiple_of(i * tile, tile), tile)
        gate = gate_up_ref[part, :]
        upper = gate_up_ref[pl.ds(pl.multiple_of(ff + i * tile, tile), tile), :]
        sig = jax.nn.sigmoid(gate)
        silu = gate * sig
        silu_ref[part, :] = silu.astype(jnp.bfloat16)
        hid_ref[part, :] = (silu * upper).astype(jnp.bfloat16)
        slope_ref[part, :] = (upper * sig * (1.0 + gate * (1.0 - sig))).astype(jnp.bfloat16)
        return carry

    lax.fori_loop(0, ff // tile, body, 0)


def make_factors(gate_up):
    whole = pl.BlockSpec(memory_space=pltpu.VMEM)
    return pl.pallas_call(
        factors_kernel,
        in_specs=[whole],
        out_specs=[whole] * 3,
        out_shape=[jax.ShapeDtypeStruct((gate_up.shape[0] // 2, gate_up.shape[1]), jnp.bfloat16)] * 3,
        compiler_params=pltpu.CompilerParams(vmem_limit_bytes=8 * 1024 * 1024),
        cost_estimate=SMALL,
        name="factors",
    )(gate_up)


def gives_kernel(table, w_ref, hid_ref, x_ref, dy_ref, slope_ref, silu_ref, dgu_ref, *refs):
    n = len(FLOWS)
    outs, stages, sems = refs[:n], refs[n : 2 * n], refs[2 * n]
    per = outs[0].shape[0]
    ff = hid_ref.shape[0]
    tile = 256
    def copy(f, chunk):
        return pltpu.make_async_copy(
            stages[f].at[:, lanes(chunk)], outs[f].at[:, lanes(chunk)], sems.at[f, chunk]
        )

    def give(f):
        def body(chunk, carry):
            for from_dgu, first, count, row in flow_parts(f, per, 2 * ff):
                left, right = (dgu_ref, x_ref) if from_dgu else (hid_ref, dy_ref)
                stages[f][row : row + count, lanes(chunk)] = product(
                    left[first : first + count, :], feature_blocks(right, table, f, chunk)
                )
            copy(f, chunk).start()
            return carry

        lax.fori_loop(0, CHUNKS, body, 0, unroll=True)

    give(3)
    for low in range(0, ff, tile):
        here = slice(low, low + tile)
        dhidden = lax.dot_general(
            w_ref[here, :], dy_ref[...], (((1,), (1,)), ((), ())), preferred_element_type=jnp.float32
        )
        dgu_ref[here, :] = (dhidden * slope_ref[here, :]).astype(jnp.bfloat16)
        dgu_ref[ff + low : ff + low + tile, :] = (dhidden * silu_ref[here, :]).astype(jnp.bfloat16)
    for f in range(3):
        give(f)
    for f in range(n):
        for chunk in range(CHUNKS):
            copy(f, chunk).wait()


def make_gives(table, w_out_t, slope, silu, hidden, rows_x, rows_dy):
    ff, rows = hidden.shape
    size = (3 * ff // 4, 2 * CHUNKS * LANE)
    whole = pl.BlockSpec(memory_space=pltpu.VMEM)
    away = pl.BlockSpec(memory_space=pl.ANY)
    n = len(FLOWS)
    return pl.pallas_call(
        gives_kernel,
        in_specs=[pl.BlockSpec(memory_space=pltpu.SMEM)] + [whole] * 6,
        out_specs=[whole] + [away] * n,
        out_shape=[jax.ShapeDtypeStruct((2 * ff, rows), jnp.bfloat16)]
        + [jax.ShapeDtypeStruct(size, jnp.bfloat16)] * n,
        scratch_shapes=[pltpu.VMEM(size, jnp.bfloat16)] * n + [pltpu.SemaphoreType.DMA((n, CHUNKS))],
        compiler_params=pltpu.CompilerParams(vmem_limit_bytes=GIVE_MIB * 1024 * 1024),
        cost_estimate=SMALL,
        name="give",
    )(table, w_out_t, hidden, rows_x, rows_dy, slope, silu)


def keeps_kernel(table, dgu_ref, hid_ref, x_ref, dy_ref, *outs):
    per = outs[0].shape[0]
    for f, out in enumerate(outs):

        def body(chunk, carry):
            for from_dgu, first, count, row in flow_parts(f, per, dgu_ref.shape[0]):
                left, right = (dgu_ref, x_ref) if from_dgu else (hid_ref, dy_ref)
                out[row : row + count, lanes(chunk)] = product(
                    left[first : first + count, :], feature_blocks(right, table, f, chunk)
                )
            return carry

        lax.fori_loop(0, CHUNKS, body, 0, unroll=True)


def make_keeps(table, dgu, hidden, rows_x, rows_dy):
    size = (3 * hidden.shape[0] // 4, 2 * CHUNKS * LANE)
    whole = pl.BlockSpec(memory_space=pltpu.VMEM)
    n = len(FLOWS)
    return pl.pallas_call(
        keeps_kernel,
        in_specs=[pl.BlockSpec(memory_space=pltpu.SMEM)] + [whole] * 4,
        out_specs=[whole] * n,
        out_shape=[jax.ShapeDtypeStruct(size, jnp.bfloat16)] * n,
        compiler_params=pltpu.CompilerParams(vmem_limit_bytes=8 * 1024 * 1024),
        cost_estimate=SMALL,
        name="keep",
    )(table, dgu, hidden, rows_x, rows_dy)


def drows_kernel(g_ref, w_ref, out_ref, turned):
    @pl.when(pl.program_id(0) == 0)
    def _():
        turned[...] = g_ref[...].T

    out_ref[...] = lax.dot_general(
        turned[...], w_ref[...], (((1,), (1,)), ((), ())), preferred_element_type=jnp.float32
    ).astype(jnp.bfloat16)


def make_drows(dgu_t, w_in):
    ff2, rows = dgu_t.shape
    width = w_in.shape[0]
    tile = 512
    return pl.pallas_call(
        drows_kernel,
        grid=(width // tile,),
        in_specs=[
            pl.BlockSpec((ff2, rows), lambda i: (0, 0)),
            pl.BlockSpec((tile, ff2), lambda i: (i, 0)),
        ],
        out_specs=pl.BlockSpec((rows, tile), lambda i: (0, i)),
        out_shape=jax.ShapeDtypeStruct((rows, width), jnp.bfloat16),
        scratch_shapes=[pltpu.VMEM((rows, ff2), jnp.bfloat16)],
        compiler_params=pltpu.CompilerParams(vmem_limit_bytes=50 * 1024 * 1024),
        cost_estimate=SMALL,
        name="drows",
    )(dgu_t, w_in)


def finish_kernel(*refs):
    *parts, up_ref, down_ref = refs
    n = len(parts) // 2
    total = jnp.concatenate(
        [parts[i][...].astype(jnp.float32) + parts[n + i][...].astype(jnp.float32) for i in range(n)], axis=0
    )
    split = up_ref.shape[1]
    up_ref[...] = total[:split].T.astype(jnp.bfloat16)
    down_ref[...] = total[split:].T.astype(jnp.bfloat16)


def finish(keeps, gots):
    per, lane = keeps[0].shape
    whole = pl.BlockSpec(memory_space=pltpu.VMEM)
    return pl.pallas_call(
        finish_kernel,
        in_specs=[whole] * 8,
        out_specs=[whole] * 2,
        out_shape=[
            jax.ShapeDtypeStruct((lane, 8 * per // 3), jnp.bfloat16),
            jax.ShapeDtypeStruct((lane, 4 * per // 3), jnp.bfloat16),
        ],
        compiler_params=pltpu.CompilerParams(vmem_limit_bytes=12 * 1024 * 1024),
        cost_estimate=FINISH,
        name="finish",
    )(*keeps, *gots)


def mate(i, odd):
    return (3 - i) if odd else (i ^ 1)


def pair_perm(axis, odd):
    return [
        (x * SIDE + y, mate(x, odd) * SIDE + y if axis == 0 else x * SIDE + mate(y, odd))
        for x in range(SIDE)
        for y in range(SIDE)
    ]


def first_table(at, axis, odd):
    a, b = at[axis], at[1 - axis]

    def kept(i):
        return [mate(i, not odd), i]

    minor = jnp.stack(kept(mate(b, odd)) + kept(b)).astype(jnp.int32)

    def blocks(i):
        major = jnp.stack(kept(i)).astype(jnp.int32)
        ids = major[:, None] * SIDE + minor[None, :] if axis == 0 else minor[None, :] * SIDE + major[:, None]
        return ids.reshape(-1)

    return blocks(mate(a, odd)), blocks(a)


def local(tokens, out_grads, expert_ids, w_gate_up, w_down_t):
    num_experts = lax.axis_size("expert")
    width = tokens.shape[1]
    ff = w_down_t.shape[2]
    rows = num_experts * SLOTS
    ids = expert_ids.reshape(1, -1)

    def send(packed):
        packed = packed.reshape(num_experts, SLOTS, width)
        got = lax.all_to_all(packed, "expert", split_axis=0, concat_axis=0, tiled=True)
        return got.reshape(rows, width)

    packed_x, target = pack(ids, tokens, num_experts)
    packed_dy, _ = pack(ids, out_grads, num_experts)
    rows_x = send(packed_x)
    rows_x, packed_dy = lax.optimization_barrier((rows_x, packed_dy))
    rows_dy = send(packed_dy)
    w_in = w_gate_up[0]
    w_out_t = w_down_t[0].T

    gate_up = lax.dot_general(
        w_in, rows_x, (((0,), (1,)), ((), ())), preferred_element_type=jnp.float32
    )
    slope, silu, hidden = make_factors(gate_up)

    me = lax.axis_index("dp")
    at = (me // SIDE, me % SIDE)
    tables = [first_table(at, axis, odd) for axis, odd in FLOWS]

    to_give = jnp.stack([t[0] for t in tables])
    to_keep = jnp.stack([t[1] for t in tables])
    dgu, *gives = make_gives(to_give, w_out_t, slope, silu, hidden, rows_x, rows_dy)
    gots = [None] * 4
    for f in (3, 0, 1, 2):
        gots[f] = lax.ppermute(gives[f], "dp", pair_perm(*FLOWS[f]))
    drows = make_drows(dgu, w_in)
    returned = lax.all_to_all(
        drows.reshape(num_experts, SLOTS, width), "expert", split_axis=0, concat_axis=0, tiled=True
    ).reshape(rows, width)
    spots = jnp.arange(rows, dtype=jnp.int32)
    token_grads = lax.dot_general(
        (spots[:, None] == target).astype(jnp.bfloat16), returned, (((0,), (0,)), ((), ())),
        preferred_element_type=jnp.float32,
    ).astype(jnp.bfloat16)

    def add_halves(keep, got):
        n = keep.shape[1] // 2
        return tuple(
            k + g
            for k, g in ((keep[:, :n], got[:, :n]), (keep[:, n:], got[:, n:]))
        )

    keeps = make_keeps(to_keep, dgu, hidden, rows_x, rows_dy)
    halves = [add_halves(keep, got) for keep, got in zip(keeps, gots)]
    for step in range(1, 4):
        for f, (first_axis, first_odd) in enumerate(FLOWS):
            axis = first_axis if step < 2 else 1 - first_axis
            odd = first_odd if step % 2 == 0 else not first_odd
            give, keep = halves[f]
            got = lax.ppermute(give, "dp", pair_perm(axis, odd))
            halves[f] = (got, keep) if step == 3 else add_halves(keep, got)
    grad_gate_up, grad_down_t = finish([h[1] for h in halves], [h[0] for h in halves])
    return (token_grads, grad_gate_up[None], grad_down_t[None])


def solution(mesh):
    return jax.shard_map(
        local,
        mesh=mesh,
        in_specs=(
            P(("dp", "expert"), None),
            P(("dp", "expert"), None),
            P(("dp", "expert"), None),
            P("expert", None, None),
            P("expert", None, None),
        ),
        out_specs=(P(("dp", "expert"), None), P("expert", "dp", None), P("expert", "dp", None)),
        check_vma=False,
    )
```
